32 devices in a mesh: groups: 2 (over x), view: 16 (over z, y, core).
Axes of the slice: x: 2, y: 2, z: 4, core: 2. Of those that a mesh axis runs over, the one named last changes fastest.
Arguments:
- images: bfloat16 [32, 4, 32, 64, 256], P(('groups', 'view')), parts along dimension 0, may hold values from 0.5 to 2
- start_estimate: float32 [512, 64, 256], P(('groups', 'view')), parts along dimension 0, may hold values from 0.5 to 1.5
- view_order: int32 [4], replicated, may hold values from 0 to 3, each once
- psf_ranks: int32 [4], replicated, may hold values from 2 to 6, as said below
- depth_taps: float32 [4, 6, 17], replicated, may hold values from 0.05 to 1
- row_taps: float32 [4, 6, 17], replicated, may hold values from 0.05 to 1
- col_taps: float32 [4, 6, 17], replicated, may hold values from 0.05 to 1
- rank_weight: float32 [4, 6], replicated, may hold values from 0.1 to 1
Outputs:
- estimate: float32 [512, 64, 256], P(('groups', 'view')), parts along dimension 0
The draws below stay inside these ranges and needn't reach their ends.
There are 2 independent parts, one for each index of `groups`. The reference program is written for one: setup_inputs(seed, part) draws one part's arguments, and reference() takes and returns one part's arrays. A program takes and returns all parts, laid end to end along the dimension named above; an argument that names none is the same for every part. Nothing has to cross between parts.
Inputs may be any that keep to these rules, and one draw needn't show every extreme that they name: `view_order`: each view appears exactly once. `psf_ranks`: some view uses 6 terms and some view uses 2.
All inputs are finite; a program needn't handle non-finite values.
Results may differ from the reference program's by a relative error of at most 0.0012.
Values sent between devices are 32-bit elements; how exact they have to be, the bound alone decides.
No kernel may reach another device: no remote copies, remote signals or barrier semaphores. Data moves between devices by JAX's collectives and lax.ppermute only.
A program may use at most 64 MiB of HBM per device.

```python
import math
import jax
import jax.numpy as jnp
from jax import lax

PLANES = 16
ROWS = 64
COLS = 256
VIEWS = 4
RANKS = 6
TAPS = 17
STEPS = 4
SLAB = 32
POSITIONS = 16
DEPTH = 256


def draw_psf_ranks(key, part):
    key = jax.random.fold_in(key, 1)
    first_key, second_key = jax.random.split(key)
    base = jax.random.randint(first_key, (VIEWS,), 2, RANKS + 1, dtype=jnp.int32)
    picked = jax.random.permutation(second_key, jnp.arange(VIEWS, dtype=jnp.int32))
    base = base.at[picked[0]].set(RANKS)
    base = base.at[picked[1]].set(2)
    return base.astype(jnp.int32)


def shard_levels(stream_key, extent, pieces, low, high):
    level = 1.0
    for dim, blocks in pieces:
        heights = jax.random.uniform(jax.random.fold_in(jax.random.fold_in(stream_key, 6), dim), (blocks,), jnp.float32, low / len(pieces), high / len(pieces))
        level = level * jnp.repeat(jnp.exp(heights), extent[dim] // blocks).reshape((-1,) + (1,) * (len(extent) - 1 - dim))
    return level


def setup_inputs(seed: int = 0, part: int = 0) -> dict:
    key_list = jax.random.split(jax.random.key(seed), 9)
    own_keys = jax.random.split(jax.random.fold_in(key_list[8], part), 9)
    return {
        "images": jnp.clip(0.5 + 1.5 * jax.random.uniform(own_keys[0], (POSITIONS, STEPS, SLAB, ROWS, COLS), jnp.float32) ** shard_levels(own_keys[0], (POSITIONS, STEPS, SLAB, ROWS, COLS), ((0, 16),), -0.2, 0.2), 0.5, 2.0).astype(jnp.bfloat16),
        "start_estimate": jnp.clip(0.5 + 1.0 * jax.random.uniform(own_keys[1], (DEPTH, ROWS, COLS), jnp.float32) ** shard_levels(own_keys[1], (DEPTH, ROWS, COLS), ((0, 16),), -0.2, 0.2), 0.5, 1.5),
        "view_order": jax.random.permutation(key_list[2], VIEWS).astype(jnp.int32),
        "psf_ranks": draw_psf_ranks(jax.random.fold_in(key_list[8], 71), part),
        "depth_taps": jnp.clip(jnp.exp(jax.random.uniform(key_list[4], (VIEWS, RANKS, TAPS), jnp.float32, math.log(0.05), math.log(1.0))), 0.05, 1.0),
        "row_taps": jnp.clip(jnp.exp(jax.random.uniform(key_list[5], (VIEWS, RANKS, TAPS), jnp.float32, math.log(0.05), math.log(1.0))), 0.05, 1.0),
        "col_taps": jnp.clip(jnp.exp(jax.random.uniform(key_list[6], (VIEWS, RANKS, TAPS), jnp.float32, math.log(0.05), math.log(1.0))), 0.05, 1.0),
        "rank_weight": jnp.clip(jnp.exp(jax.random.uniform(key_list[7], (VIEWS, RANKS), jnp.float32, math.log(0.1), math.log(1.0))), 0.1, 1.0),
    }


def to_half(values):
    return lax.optimization_barrier(values.astype(jnp.bfloat16)).astype(jnp.float32)


def banded(taps, n_out, n_in, sign, offset):
    rows_out = jnp.arange(n_out, dtype=jnp.int32)[:, None]
    cols_in = jnp.arange(n_in, dtype=jnp.int32)[None, :]
    distance = sign * (cols_in - rows_out) + offset
    picks = (distance[:, :, None] == jnp.arange(taps.shape[-1], dtype=jnp.int32)[None, None, :]).astype(jnp.float32)
    return jnp.einsum("oik,rk->roi", picks, taps, precision=lax.Precision.HIGHEST)


def kernels(view_id, depth_taps, row_taps, col_taps, rank_weight, psf_ranks):
    live = (jnp.arange(depth_taps.shape[1], dtype=jnp.int32) < psf_ranks[view_id]).astype(jnp.float32)
    weights = rank_weight[view_id] * live
    weights = weights / jnp.sum(weights)
    depth_factor = depth_taps[view_id] / jnp.sum(depth_taps[view_id], axis=1, keepdims=True) * weights[:, None]
    row_factor = row_taps[view_id] / jnp.sum(row_taps[view_id], axis=1, keepdims=True)
    col_factor = col_taps[view_id] / jnp.sum(col_taps[view_id], axis=1, keepdims=True)
    return to_half(depth_factor), to_half(row_factor), to_half(col_factor)


def operators(depth_factor, row_factor, col_factor, planes, row_count, col_count):
    margin = depth_factor.shape[1] // 2
    forward_depth = banded(depth_factor, planes + 2 * margin, planes + 4 * margin, 1, 0)
    forward_rows = banded(row_factor, row_count, row_count, 1, margin)
    forward_cols = banded(col_factor, col_count, col_count, 1, margin)
    adjoint_depth = banded(depth_factor, planes, planes + 2 * margin, -1, 2 * margin)
    adjoint_rows = banded(row_factor, row_count, row_count, -1, margin)
    adjoint_cols = banded(col_factor, col_count, col_count, -1, margin)
    return forward_depth, forward_rows, forward_cols, adjoint_depth, adjoint_rows, adjoint_cols


def refine(extended, observed, banded_ops):
    forward_depth, forward_rows, forward_cols, adjoint_depth, adjoint_rows, adjoint_cols = banded_ops
    highest = lax.Precision.HIGHEST
    extended = to_half(extended)
    partial_blur = to_half(jnp.einsum("rqz,zyx->rqyx", forward_depth, extended, precision=highest))
    partial_blur = to_half(jnp.einsum("ryv,rqvx->rqyx", forward_rows, partial_blur, precision=highest))
    blurred = jnp.einsum("rqyx,rwx->qyw", partial_blur, forward_cols, precision=highest)
    ratio = to_half(observed / blurred)
    partial_back = to_half(jnp.einsum("rmq,qyx->rmyx", adjoint_depth, ratio, precision=highest))
    partial_back = to_half(jnp.einsum("ryv,rmvx->rmyx", adjoint_rows, partial_back, precision=highest))
    return jnp.einsum("rmyx,rwx->myw", partial_back, adjoint_cols, precision=highest)


def reference(images, start_estimate, view_order, psf_ranks, depth_taps, row_taps, col_taps, rank_weight):
    margin = TAPS // 2
    position_count = images.shape[0]
    view_count = view_order.shape[0]
    depth = start_estimate.shape[0]

    def one_step(estimate, step_index):
        padded = jnp.pad(estimate, ((2 * margin, 2 * margin), (0, 0), (0, 0)))

        def one_block(block_index):
            position = ((block_index + step_index) % position_count).astype(jnp.int32)
            view_id = view_order[position % view_count]
            depth_factor, row_factor, col_factor = kernels(view_id, depth_taps, row_taps, col_taps, rank_weight, psf_ranks)
            banded_ops = operators(depth_factor, row_factor, col_factor, PLANES, ROWS, COLS)
            start_plane = (block_index * PLANES).astype(jnp.int32)
            extended = lax.dynamic_slice_in_dim(padded, start_plane, PLANES + 4 * margin, 0)
            zero_index = jnp.zeros((), jnp.int32)
            observed = lax.dynamic_slice(images, (position, step_index.astype(jnp.int32), zero_index, zero_index, zero_index), (1, 1, PLANES + 2 * margin, ROWS, COLS))[0, 0]
            plane_ids = start_plane - margin + jnp.arange(PLANES + 2 * margin, dtype=jnp.int32)
            inside = (plane_ids >= 0) & (plane_ids < depth)
            observed = jnp.where(inside[:, None, None], observed.astype(jnp.float32), jnp.zeros((), jnp.float32))
            own_block = lax.dynamic_slice_in_dim(estimate, start_plane, PLANES, 0)
            return own_block * refine(extended, observed, banded_ops)

        blocks = lax.map(one_block, jnp.arange(position_count, dtype=jnp.int32))
        return blocks.reshape(estimate.shape), None

    final, unused = lax.scan(one_step, start_estimate, jnp.arange(STEPS, dtype=jnp.int32))
    return final
```

```python
import jax
import jax.numpy as jnp
from jax import lax
from jax.experimental import pallas as pl
from jax.experimental.pallas import tpu as pltpu
from jax.sharding import PartitionSpec as P

STEPS = 4
ROW_GROUP = 8
PLANE_GROUP = 4

F32 = jnp.float32
BF16 = jnp.bfloat16


def dot(a, b):
    return jnp.dot(a, b, preferred_element_type=F32)


def factors(view_id, depth_taps, row_taps, col_taps, rank_weight, psf_ranks):
    live = (jnp.arange(depth_taps.shape[1], dtype=jnp.int32) < psf_ranks[view_id]).astype(F32)
    weights = rank_weight[view_id] * live
    weights = weights / jnp.sum(weights)
    depth = depth_taps[view_id]
    row = row_taps[view_id]
    col = col_taps[view_id]
    depth = depth / jnp.sum(depth, axis=1, keepdims=True) * weights[:, None]
    row = row / jnp.sum(row, axis=1, keepdims=True)
    col = col / jnp.sum(col, axis=1, keepdims=True)
    return jnp.stack([depth, row, col])


def build_kernel(taps, depth_f, depth_a, row_f, row_a, col_f, col_a):
    ranks = depth_f.shape[0]
    count = taps.shape[2]
    margin = count // 2

    def toeplitz(kind, r, dist, scale):
        total = jnp.zeros(dist.shape, F32)
        for k in range(count):
            total = jnp.where(dist == scale * k, taps[kind, r, k], total)
        return total

    def diff(n, m):
        return lax.broadcasted_iota(jnp.int32, (n, m), 1) - lax.broadcasted_iota(
            jnp.int32, (n, m), 0
        )

    def one(r, carry):
        d = diff(depth_f.shape[1], depth_f.shape[2])
        depth_f[r] = toeplitz(0, r, d, ROW_GROUP).astype(BF16)
        depth_a[r] = toeplitz(0, r, ROW_GROUP * (count - 1) - d, ROW_GROUP).astype(BF16)
        n = col_f.shape[1]
        d = diff(n, n)
        col_a[r] = toeplitz(2, r, d + margin, 1).astype(BF16)
        col_f[r] = toeplitz(2, r, margin - d, 1).astype(BF16)
        n = row_f.shape[1]
        d = diff(n, n)
        rows = n // PLANE_GROUP
        same = lax.broadcasted_iota(jnp.int32, (n, n), 0) // rows == (
            lax.broadcasted_iota(jnp.int32, (n, n), 1) // rows
        )
        d = jnp.where(same, d, n)
        row_f[r] = toeplitz(1, r, d + margin, 1).astype(BF16)
        row_a[r] = toeplitz(1, r, margin - d, 1).astype(BF16)
        return carry

    lax.fori_loop(0, ranks, one, 0)


def build(taps, planes, rows, cols):
    ranks = taps.shape[1]
    depth = jax.ShapeDtypeStruct((ranks, planes * ROW_GROUP, 2 * planes * ROW_GROUP), BF16)
    row = jax.ShapeDtypeStruct((ranks, PLANE_GROUP * rows, PLANE_GROUP * rows), BF16)
    col = jax.ShapeDtypeStruct((ranks, cols, cols), BF16)
    return pl.pallas_call(
        build_kernel,
        out_shape=[depth, depth, row, row, col, col],
        in_specs=[pl.BlockSpec(memory_space=pltpu.SMEM)],
        out_specs=[pl.BlockSpec(memory_space=pltpu.VMEM)] * 6,
        compiler_params=pltpu.CompilerParams(vmem_limit_bytes=24 * 2**20),
        name="build",
    )(taps)


def depth_pass(first, second, op, out, start, scale=None):
    ranks = op.shape[0]
    planes, rows, cols = first.shape
    step = 2 * ROW_GROUP

    def one(i, carry):
        tiles = []
        for half in range(2):
            y = pl.ds(pl.multiple_of(i * step + half * ROW_GROUP, ROW_GROUP), ROW_GROUP)
            tail = second[:, y, :] if scale is None else second[:, y, :] * scale
            both = jnp.concatenate([first[:, y, :], tail], axis=0)
            tiles.append(both.reshape(2 * planes * ROW_GROUP, cols).astype(BF16))
        y = pl.ds(pl.multiple_of(i * step, step), step)
        for r in range(ranks):
            parts = [dot(op[r], tile).reshape(planes, ROW_GROUP, cols) for tile in tiles]
            out[r, pl.ds(start, planes), y, :] = jnp.concatenate(parts, axis=1).astype(BF16)
        return carry

    lax.fori_loop(0, rows // step, one, 0)


def row_pass(src, op, out, planes):
    ranks, _, rows, cols = src.shape
    size = PLANE_GROUP * rows

    def one(i, carry):
        at = pl.multiple_of(i * size, size)
        for r in range(ranks):
            data = src[r, pl.ds(i * PLANE_GROUP, PLANE_GROUP)].reshape(size, cols)
            out[pl.ds(at, size), r * cols : (r + 1) * cols] = dot(op[r], data).astype(BF16)
        return carry

    lax.fori_loop(0, planes // PLANE_GROUP, one, 0)


def col_pass(src, op, planes, rows, finish):
    ranks, cols, _ = op.shape
    size = PLANE_GROUP * rows
    weights = op[...].reshape(ranks * cols, cols)

    def one(i, carry):
        at = pl.multiple_of(i * size, size)
        result = dot(src[pl.ds(at, size), :], weights)
        finish(i * PLANE_GROUP, result.reshape(PLANE_GROUP, rows, cols))
        return carry

    lax.fori_loop(0, planes // PLANE_GROUP, one, 0)


def step_kernel(
    step,
    margin,
    block,
    below,
    own,
    above,
    images,
    depth_f,
    depth_a,
    row_f,
    row_a,
    col_f,
    col_a,
    out,
    spread,
    mixed,
    ratio,
    observed,
    sem,
):
    planes, rows, cols = own.shape
    slab = observed.shape[0]
    copy = pltpu.make_async_copy(images.at[0, step], observed, sem)
    copy.start()

    depth_pass(below, own, depth_f, spread, 0)
    depth_pass(own, above, depth_f, spread, planes, block[1].astype(F32))
    row_pass(spread, row_f, mixed, slab)
    copy.wait()

    def to_ratio(q, blurred):
        z = lax.broadcasted_iota(jnp.int32, (PLANE_GROUP, 1, 1), 0) + (
            q + block[0] * planes - margin
        )
        inside = (z >= 0) & (z < block[2] * planes)
        seen = observed[pl.ds(q, PLANE_GROUP)].astype(F32)
        value = jnp.where(inside, seen, 0.0) / blurred
        ratio[pl.ds(q, PLANE_GROUP)] = value

    col_pass(mixed, col_f, slab, rows, to_ratio)
    depth_pass(ratio.at[pl.ds(0, planes)], ratio.at[pl.ds(planes, planes)], depth_a, spread, 0)
    row_pass(spread, row_a, mixed, planes)

    def to_update(m, back):
        at = pl.ds(m, PLANE_GROUP)
        out[at] = own[at] * back

    col_pass(mixed, col_a, planes, rows, to_update)


def refine(step, margin, block, below, own, above, images, ops):
    planes, rows, cols = own.shape
    ranks = ops[0].shape[0]
    slab = images.shape[2]
    vmem = pl.BlockSpec(memory_space=pltpu.VMEM)

    def kernel(*refs):
        step_kernel(step, margin, *refs)

    return pl.pallas_call(
        kernel,
        out_shape=jax.ShapeDtypeStruct(own.shape, F32),
        in_specs=[pl.BlockSpec(memory_space=pltpu.SMEM)]
        + [vmem] * 3
        + [pl.BlockSpec(memory_space=pl.ANY)]
        + [vmem] * 6,
        out_specs=vmem,
        scratch_shapes=[
            pltpu.VMEM((ranks, slab, rows, cols), BF16),
            pltpu.VMEM((slab * rows, ranks * cols), BF16),
            pltpu.VMEM((slab, rows, cols), F32),
            pltpu.VMEM((slab, rows, cols), BF16),
            pltpu.SemaphoreType.DMA,
        ],
        compiler_params=pltpu.CompilerParams(vmem_limit_bytes=44 * 2**20),
        name="refine",
    )(block, below, own, above, images, *ops)


def shards(
    images, start_estimate, view_order, psf_ranks, depth_taps, row_taps, col_taps, rank_weight
):
    margin = depth_taps.shape[2] // 2
    count = lax.axis_size("view")
    position = lax.axis_index("view")
    planes, rows, cols = start_estimate.shape

    def send(cells, by, skip=()):
        pairs = [(i, (i + by) % count) for i in range(count) if i not in skip]
        return lax.ppermute(cells, "view", pairs)

    own = start_estimate
    below = send(own, 1, (count - 1,))
    above = send(own, -1, (0,))

    view_id = view_order[position % view_order.shape[0]]
    taps = factors(view_id, depth_taps, row_taps, col_taps, rank_weight, psf_ranks)
    ops = build(taps.astype(BF16).astype(F32), planes, rows, cols)

    for step in range(STEPS):
        block = (position - step) % count
        facts = jnp.stack(
            [block, (block < count - 1).astype(jnp.int32), jnp.int32(count)]
        ).astype(jnp.int32)
        updated = refine(step, margin, facts, below, own, above, images, ops)
        if step < STEPS - 1:
            own = send(updated, 1)
            below = send(own, 1, (step,))
            above = updated
    return send(updated, -(STEPS - 1))


def solution(mesh):
    in_specs = (
        P(("groups", "view"), None, None, None, None),
        P(("groups", "view"), None, None),
        P(),
        P(),
        P(),
        P(),
        P(),
        P(),
    )
    out_specs = P(("groups", "view"), None, None)
    return jax.shard_map(shards, mesh=mesh, in_specs=in_specs, out_specs=out_specs, check_vma=False)
```

```python
import jax
import jax.numpy as jnp
from jax import lax
from jax.experimental import pallas as pl
from jax.experimental.pallas import tpu as pltpu
from jax.sharding import PartitionSpec as P

STEPS = 4
PLANES = 16
HALF = 8
ROWS = 64
COLS = 256
GROUP = 8
QUAD = 4
TILE = 256

F32 = jnp.float32
BF16 = jnp.bfloat16
VMEM = pl.BlockSpec(memory_space=pltpu.VMEM)
SMEM = pl.BlockSpec(memory_space=pltpu.SMEM)
ANY = pl.BlockSpec(memory_space=pl.ANY)


def dot(a, b):
    return jnp.dot(a, b, preferred_element_type=F32)


def iota(shape, dim):
    return lax.broadcasted_iota(jnp.int32, shape, dim)


def build_kernel(
    order, live, weight, depth_taps, row_taps, col_taps,
    depth_f, depth_a, row_f, row_a, col_f, col_a, held,
):
    views = order.shape[0]
    ranks, count = depth_taps.shape[1:]
    margin = count // 2
    view = order[lax.rem(lax.axis_index("view"), views)]
    square = (TILE, TILE)

    def normal(taps):
        values = taps[view]
        return values / jnp.sum(values, axis=1, keepdims=True)

    rank = iota((ranks, 1), 0)
    weights = jnp.zeros((ranks, 1), F32)
    for r in range(ranks):
        weights = jnp.where(rank == r, weight[view, r], weights)
    weights = jnp.where(rank < live[view], weights, 0.0)
    weights = weights / jnp.sum(weights, axis=0, keepdims=True)

    def placed(values, place):
        held[...] = jnp.zeros(held.shape, F32)
        held[0:ranks, 0:count] = values
        k = iota((held.shape[1], TILE), 0)
        picks = (k < count) & (iota((held.shape[1], TILE), 1) == place(k))
        return dot(held[...].astype(BF16), picks.astype(F32).astype(BF16))

    def rolled(rows, r, n):
        full = jnp.broadcast_to(rows[r : r + 1], (n, TILE))
        return pltpu.roll(full, 0, 1, stride=1, stride_axis=0)

    depth = normal(depth_taps) * weights
    ahead = placed(depth, lambda k: GROUP * k)
    back = placed(depth, lambda k: GROUP * (count - 1 - k))
    for r in range(ranks):
        depth_f[r] = rolled(ahead, r, PLANES * GROUP).astype(BF16)
        depth_a[r] = rolled(back, r, PLANES * GROUP).astype(BF16)

    i, j = iota(square, 0), iota(square, 1)
    near = jnp.abs(j - i) <= margin
    col = normal(col_taps)
    ahead = placed(col, lambda k: (margin - k) & (TILE - 1))
    back = placed(col, lambda k: (k - margin) & (TILE - 1))
    for r in range(ranks):
        col_f[r] = jnp.where(near, rolled(ahead, r, TILE), 0.0).astype(BF16)
        col_a[r] = jnp.where(near, rolled(back, r, TILE), 0.0).astype(BF16)

    near = near & ((i >> 6) == (j >> 6))
    place = ROWS * ((j >> 3) & (QUAD - 1)) + GROUP * (j >> 5) + (j & (GROUP - 1))
    order_columns = (i == place).astype(F32).astype(BF16)
    row = normal(row_taps)
    ahead = placed(row, lambda k: (k - margin) & (TILE - 1))
    back = placed(row, lambda k: (margin - k) & (TILE - 1))
    for r in range(ranks):
        band = jnp.where(near, rolled(ahead, r, TILE), 0.0).astype(BF16)
        row_f[r] = dot(band, order_columns).astype(BF16)
        band = jnp.where(near, rolled(back, r, TILE), 0.0).astype(BF16)
        row_a[r] = dot(band, order_columns).astype(BF16)


def build(view_order, psf_ranks, rank_weight, depth_taps, row_taps, col_taps):
    ranks = depth_taps.shape[1]
    depth = jax.ShapeDtypeStruct((ranks, PLANES * GROUP, TILE), BF16)
    square = jax.ShapeDtypeStruct((ranks, TILE, TILE), BF16)
    return pl.pallas_call(
        build_kernel,
        out_shape=[depth, depth] + [square] * 4,
        in_specs=[SMEM] * 3 + [VMEM] * 3,
        out_specs=[VMEM] * 6,
        scratch_shapes=[pltpu.VMEM((8, 128), F32)],
        compiler_params=pltpu.CompilerParams(vmem_limit_bytes=16 * 2**20),
        name="build",
    )(view_order, psf_ranks, rank_weight, depth_taps, row_taps, col_taps)


def blur(pieces, ops, spread, mixed, planes):
    depth, row, col = ops
    ranks = depth.shape[0]
    lhs = depth[:, 0 : planes * GROUP, :].reshape(ranks * planes * GROUP, TILE)
    for g in range(ROWS // GROUP):
        y = slice(g * GROUP, (g + 1) * GROUP)
        cells = jnp.concatenate([piece(y) for piece in pieces], axis=0)
        cells = cells.reshape(TILE, COLS).astype(BF16)
        out = dot(lhs, cells).astype(BF16)
        out = out.reshape(ranks, planes // QUAD, QUAD * GROUP, COLS)
        spread[:, 0 : planes // QUAD, g * QUAD * GROUP : (g + 1) * QUAD * GROUP, :] = out
    for t in range(planes // QUAD):
        for r in range(ranks):
            mixed[t * TILE : (t + 1) * TILE, r * COLS : (r + 1) * COLS] = dot(
                row[r], spread[r, t]
            ).astype(BF16)
    return dot(mixed[0 : planes * ROWS, :], col[...].reshape(ranks * COLS, COLS))


def reader(ref, start, scale=None):
    def read(y):
        cells = ref[start : start + HALF, y, :]
        return cells if scale is None else cells * scale

    return read


def ratio_of(blurred, observed, q, block, count):
    planes = observed.shape[0]
    blurred = blurred.reshape(planes, ROWS, COLS)
    z = iota((planes, 1, 1), 0) + (q + block * PLANES - HALF)
    inside = (z >= 0) & (z < count * PLANES)
    return jnp.where(inside, observed[...].astype(F32), 0.0) / blurred


def block_of(step):
    count = lax.axis_size("view")
    return lax.rem(lax.axis_index("view") + (count - step), count), count


def call(kernel, name, step, arrays, images, ops, outs, planes, work):
    ranks = ops[0].shape[0]
    out = [jax.ShapeDtypeStruct((n, ROWS, COLS), F32) for n in outs]
    flops = work * ROWS * ranks * 3 * 2 * TILE * TILE
    return pl.pallas_call(
        kernel,
        out_shape=out,
        in_specs=[VMEM] * len(arrays) + [ANY] + [VMEM] * len(ops),
        out_specs=[VMEM] * len(out),
        scratch_shapes=[
            pltpu.VMEM((ranks, planes // QUAD, TILE, COLS), BF16),
            pltpu.VMEM((planes * ROWS, ranks * COLS), BF16),
            pltpu.VMEM((planes, ROWS, COLS), BF16),
            pltpu.SemaphoreType.DMA,
        ],
        compiler_params=pltpu.CompilerParams(vmem_limit_bytes=20 * 2**20),
        cost_estimate=pl.CostEstimate(flops=flops, bytes_accessed=2**20, transcendentals=0),
        name=name,
    )(*arrays, images, *ops)


def upper_ratio(step, own, above, images, ops):
    offsets = [at for _, at in own + above]

    def kernel(*refs):
        block, count = block_of(step)
        own_lo, own_hi, above_lo, above_hi, images, depth, row, col = refs[:8]
        ratio, spread, mixed, observed, sem = refs[8:]
        copy = pltpu.make_async_copy(images.at[0, step, pl.ds(PLANES, PLANES)], observed, sem)
        copy.start()
        scale = (block < count - 1).astype(F32)
        pieces = [
            reader(own_lo, offsets[0]),
            reader(own_hi, offsets[1]),
            reader(above_lo, offsets[2], scale),
            reader(above_hi, offsets[3], scale),
        ]
        blurred = blur(pieces, (depth, row, col), spread, mixed, PLANES)
        copy.wait()
        ratio[...] = ratio_of(blurred, observed, PLANES, block, count)

    arrays = [a for a, _ in own + above]
    return call(kernel, "upper", step, arrays, images, ops[0::2], [PLANES], PLANES, PLANES)[0]


def upper_update(step, below_hi, own, ratio_up, images, ops):
    offsets = [below_hi[1]] + [at for _, at in own]

    def kernel(*refs):
        block, count = block_of(step)
        below_hi, own_lo, own_hi, ratio_up, images = refs[:5]
        depth_f, depth_a, row_f, row_a, col_f, col_a = refs[5:11]
        ratio, updated, spread, mixed, observed, sem = refs[11:]
        copy = pltpu.make_async_copy(images.at[0, step, pl.ds(HALF, HALF)], observed, sem)
        copy.start()
        own_top = reader(own_hi, offsets[2])
        pieces = [reader(below_hi, offsets[0]), reader(own_lo, offsets[1]), own_top, own_top]
        blurred = blur(pieces, (depth_f, row_f, col_f), spread, mixed, HALF)
        copy.wait()
        ratio[...] = ratio_of(blurred, observed, HALF, block, count)
        top = reader(ratio_up, HALF)
        pieces = [reader(ratio, 0), reader(ratio_up, 0), top, top]
        back = blur(pieces, (depth_a, row_a, col_a), spread, mixed, HALF)
        at = slice(offsets[2], offsets[2] + HALF)
        updated[...] = own_hi[at] * back.reshape(HALF, ROWS, COLS)

    arrays = [below_hi[0]] + [a for a, _ in own] + [ratio_up]
    return call(kernel, "middle", step, arrays, images, ops, [HALF, HALF], HALF, 2 * HALF)


def lower_update(step, below, own_lo, ratio_mid, ratio_up, images, ops):
    offsets = [at for _, at in below] + [own_lo[1]]

    def kernel(*refs):
        block, count = block_of(step)
        below_lo, below_hi, own_lo, ratio_mid, ratio_up, images = refs[:6]
        depth_f, depth_a, row_f, row_a, col_f, col_a = refs[6:12]
        updated, spread, mixed, observed, sem, ratio = refs[12:]
        copy = pltpu.make_async_copy(images.at[0, step, pl.ds(0, HALF)], observed, sem)
        copy.start()
        own_low = reader(own_lo, offsets[2])
        pieces = [reader(below_lo, offsets[0]), reader(below_hi, offsets[1]), own_low, own_low]
        blurred = blur(pieces, (depth_f, row_f, col_f), spread, mixed, HALF)
        copy.wait()
        ratio[...] = ratio_of(blurred, observed, 0, block, count)
        top = reader(ratio_up, 0)
        pieces = [reader(ratio, 0), reader(ratio_mid, 0), top, top]
        back = blur(pieces, (depth_a, row_a, col_a), spread, mixed, HALF)
        at = slice(offsets[2], offsets[2] + HALF)
        updated[...] = own_lo[at] * back.reshape(HALF, ROWS, COLS)

    def wrapped(*refs):
        pl.run_scoped(lambda ratio: kernel(*refs, ratio), pltpu.VMEM((HALF, ROWS, COLS), F32))

    arrays = [a for a, _ in below] + [own_lo[0], ratio_mid, ratio_up]
    return call(wrapped, "lower", step, arrays, images, ops, [HALF], HALF, 2 * HALF)[0]


def shards(
    images, start_estimate, view_order, psf_ranks, depth_taps, row_taps, col_taps, rank_weight
):
    count = lax.axis_size("view")

    def send(cells, by, skip=()):
        pairs = [(i, (i + by) % count) for i in range(count) if i not in skip]
        return lax.ppermute(cells, "view", pairs)

    start_lo, start_hi = start_estimate[:HALF], start_estimate[HALF:]
    above_lo = send(start_lo, -1, (0,))
    above_hi = send(start_hi, -1, (0,))
    ops = build(view_order, psf_ranks, rank_weight, depth_taps, row_taps, col_taps)
    start_hi, start_lo, _ = lax.optimization_barrier((start_hi, start_lo, ops[0]))
    below_hi = send(start_hi, 1, (count - 1,))
    below_lo = send(start_lo, 1, (count - 1,))

    own = [(start_estimate, 0), (start_estimate, HALF)]
    for step in range(STEPS):
        above = [(above_lo, 0), (above_hi, 0)]
        ratio_up = upper_ratio(step, own, above, images, ops)
        ratio_mid, above_hi = upper_update(step, (below_hi, 0), own, ratio_up, images, ops)
        last = step == STEPS - 1
        own_hi = send(above_hi, 1 - STEPS if last else 1)
        below = [(below_lo, 0), (below_hi, 0)]
        above_lo = lower_update(step, below, own[0], ratio_mid, ratio_up, images, ops)
        own_lo = send(above_lo, 1 - STEPS if last else 1)
        if not last:
            below_hi = send(own_hi, 1, (step,))
            below_lo = send(own_lo, 1, (step,))
            own = [(own_lo, 0), (own_hi, 0)]
    return jnp.concatenate([own_lo, own_hi], axis=0)


def solution(mesh):
    in_specs = (
        P(("groups", "view"), None, None, None, None),
        P(("groups", "view"), None, None),
        P(),
        P(),
        P(),
        P(),
        P(),
        P(),
    )
    out_specs = P(("groups", "view"), None, None)
    return jax.shard_map(shards, mesh=mesh, in_specs=in_specs, out_specs=out_specs, check_vma=False)
```

```python
import jax
import jax.numpy as jnp
from jax import lax
from jax.experimental import pallas as pl
from jax.experimental.pallas import tpu as pltpu
from jax.sharding import PartitionSpec as P

STEPS = 4
PLANES = 16
MARGIN = 8
SIZES = (4, 4, 4, 4)
ROWS = 64
COLS = 256
GROUP = 8
QUAD = 4
TILE = 256

F32 = jnp.float32
BF16 = jnp.bfloat16
VMEM = pl.BlockSpec(memory_space=pltpu.VMEM)
SMEM = pl.BlockSpec(memory_space=pltpu.SMEM)
COST = pl.CostEstimate(flops=2**20, bytes_accessed=2**10, transcendentals=0)
HBM = pl.BlockSpec(memory_space=pltpu.HBM)


def dot(a, b):
    return jnp.dot(a, b, preferred_element_type=F32)


def iota(shape, dim):
    return lax.broadcasted_iota(jnp.int32, shape, dim)


def build_kernel(
    order, live, weight, depth_taps, row_taps, col_taps, images,
    depth_f, depth_a, row_f, row_a, col_f, col_a, slabs, held, sem,
):
    copy = pltpu.make_async_copy(images.at[0], slabs, sem)
    copy.start()
    views = order.shape[0]
    ranks, count = depth_taps.shape[1:]
    margin = count // 2
    view = order[lax.rem(lax.axis_index("view"), views)]
    square = (TILE, TILE)

    def normal(taps):
        values = taps[view]
        return values / jnp.sum(values, axis=1, keepdims=True)

    rank = iota((ranks, 1), 0)
    weights = jnp.zeros((ranks, 1), F32)
    for r in range(ranks):
        weights = jnp.where(rank == r, weight[view, r], weights)
    weights = jnp.where(rank < live[view], weights, 0.0)
    weights = weights / jnp.sum(weights, axis=0, keepdims=True)

    def placed(values, place):
        held[...] = jnp.zeros(held.shape, F32)
        held[0:ranks, 0:count] = values
        k = iota((held.shape[1], TILE), 0)
        picks = (k < count) & (iota((held.shape[1], TILE), 1) == place(k))
        return dot(held[...].astype(BF16), picks.astype(F32).astype(BF16))

    def rolled(rows, r, n):
        full = jnp.broadcast_to(rows[r : r + 1], (n, TILE))
        return pltpu.roll(full, 0, 1, stride=1, stride_axis=0)

    depth = normal(depth_taps) * weights
    ahead = placed(depth, lambda k: GROUP * k)
    back = placed(depth, lambda k: GROUP * (count - 1 - k))
    for r in range(ranks):
        depth_f[r] = rolled(ahead, r, PLANES * GROUP).astype(BF16)
        depth_a[r] = rolled(back, r, PLANES * GROUP).astype(BF16)

    i, j = iota(square, 0), iota(square, 1)
    near = jnp.abs(j - i) <= margin
    col = normal(col_taps)
    ahead = placed(col, lambda k: (margin - k) & (TILE - 1))
    back = placed(col, lambda k: (k - margin) & (TILE - 1))
    for r in range(ranks):
        col_f[r] = jnp.where(near, rolled(ahead, r, TILE), 0.0).astype(BF16)
        col_a[r] = jnp.where(near, rolled(back, r, TILE), 0.0).astype(BF16)

    near = near & ((i >> 6) == (j >> 6))
    place = ROWS * ((j >> 3) & (QUAD - 1)) + GROUP * (j >> 5) + (j & (GROUP - 1))
    order_columns = (i == place).astype(F32).astype(BF16)
    row = normal(row_taps)
    ahead = placed(row, lambda k: (k - margin) & (TILE - 1))
    back = placed(row, lambda k: (margin - k) & (TILE - 1))
    for r in range(ranks):
        band = jnp.where(near, rolled(ahead, r, TILE), 0.0).astype(BF16)
        row_f[r] = dot(band, order_columns).astype(BF16)
        band = jnp.where(near, rolled(back, r, TILE), 0.0).astype(BF16)
        row_a[r] = dot(band, order_columns).astype(BF16)
    copy.wait()


def build(view_order, psf_ranks, rank_weight, depth_taps, row_taps, col_taps, images):
    ranks = depth_taps.shape[1]
    depth = jax.ShapeDtypeStruct((ranks, PLANES * GROUP, TILE), BF16)
    square = jax.ShapeDtypeStruct((ranks, TILE, TILE), BF16)
    slabs = jax.ShapeDtypeStruct(images.shape[1:], BF16)
    *ops, slabs = pl.pallas_call(
        build_kernel,
        out_shape=[depth, depth] + [square] * 4 + [slabs],
        in_specs=[SMEM] * 3 + [VMEM] * 3 + [HBM],
        out_specs=[VMEM] * 7,
        scratch_shapes=[pltpu.VMEM((8, 128), F32), pltpu.SemaphoreType.DMA],
        compiler_params=pltpu.CompilerParams(vmem_limit_bytes=20 * 2**20),
        name="build",
    )(view_order, psf_ranks, rank_weight, depth_taps, row_taps, col_taps, images)
    return ops, slabs


def blur(cells_of, ops, spread, mixed, planes):
    depth, row, col = ops
    ranks = depth.shape[0]
    lhs = depth[:, 0 : planes * GROUP, :].reshape(ranks * planes * GROUP, TILE)
    for g in range(ROWS // GROUP):
        cells = cells_of(slice(g * GROUP, (g + 1) * GROUP))
        out = dot(lhs, cells.reshape(TILE, COLS).astype(BF16)).astype(BF16)
        out = out.reshape(ranks, planes // QUAD, QUAD * GROUP, COLS)
        spread[:, 0 : planes // QUAD, g * QUAD * GROUP : (g + 1) * QUAD * GROUP, :] = out
    for t in range(planes // QUAD):
        for r in range(ranks):
            mixed[t * TILE : (t + 1) * TILE, r * COLS : (r + 1) * COLS] = dot(
                row[r], spread[r, t]
            ).astype(BF16)
    return dot(mixed[0 : planes * ROWS, :], col[...].reshape(ranks * COLS, COLS))


def window(refs, scales=None):
    def read(y):
        parts, left = [], 2 * PLANES
        for i, (ref, at) in enumerate(refs):
            n = min(left, ref.shape[0] - at)
            cells = ref[at : at + n, y, :]
            if scales is not None and scales[i] is not None:
                cells = cells * scales[i]
            parts.append(cells)
            left -= n
        while left > 0:
            n = min(left, parts[0].shape[0])
            parts.append(parts[0][:n])
            left -= n
        return jnp.concatenate(parts, axis=0)

    return read


def ratio_of(blurred, slab, q, planes, block, count):
    blurred = blurred.reshape(planes, ROWS, COLS)
    z = iota((planes, 1, 1), 0) + (q + block * PLANES - MARGIN)
    inside = (z >= 0) & (z < count * PLANES)
    return jnp.where(inside, slab[q : q + planes].astype(F32), 0.0) / blurred


def block_of(step):
    count = lax.axis_size("view")
    return lax.rem(lax.axis_index("view") + (count - step), count), count


def call(kernel, name, arrays, slabs, ops, outs, planes):
    ranks = ops[0].shape[0]
    out = [jax.ShapeDtypeStruct((n, ROWS, COLS), F32) for n in outs]
    return pl.pallas_call(
        kernel,
        out_shape=out,
        in_specs=[VMEM] * (len(arrays) + 1 + len(ops)),
        out_specs=[VMEM] * len(out),
        scratch_shapes=[
            pltpu.VMEM((ranks, planes // QUAD, TILE, COLS), BF16),
            pltpu.VMEM((planes * ROWS, ranks * COLS), BF16),
        ],
        compiler_params=pltpu.CompilerParams(vmem_limit_bytes=20 * 2**20),
        cost_estimate=COST,
        name=name,
    )(*arrays, slabs, *ops)


def upper_ratio(step, own, above, slabs, ops):
    def kernel(*refs):
        block, count = block_of(step)
        refs = list(refs)
        own_refs = [refs.pop(0) for _ in own]
        above_refs = [refs.pop(0) for _ in above]
        slabs, depth, row, col, ratio, spread, mixed = refs
        scale = (block < count - 1).astype(F32)
        scales = [None] * len(own) + [scale] * len(above)
        cells = window([(ref, 0) for ref in own_refs + above_refs], scales)
        blurred = blur(cells, (depth, row, col), spread, mixed, PLANES)
        ratio[...] = ratio_of(blurred, slabs.at[step], PLANES, PLANES, block, count)

    arrays = own + above
    return call(kernel, "upper", arrays, slabs, ops[0::2], [PLANES], PLANES)[0]


def piece_update(step, index, below, own, ratios, ratio_up, slabs, ops):
    n = own[-1].shape[0]
    start = sum(SIZES[index + 1 :])

    def kernel(*refs):
        block, count = block_of(step)
        refs = list(refs)
        below_refs = [refs.pop(0) for _ in below]
        own_refs = [refs.pop(0) for _ in own]
        ratio_refs = [refs.pop(0) for _ in ratios]
        ratio_up, slabs = refs[:2]
        depth_f, depth_a, row_f, row_a, col_f, col_a = refs[2:8]
        ratio, updated, spread, mixed = refs[8:]
        cells = window([(ref, 0) for ref in below_refs + own_refs])
        blurred = blur(cells, (depth_f, row_f, col_f), spread, mixed, n)
        ratio[...] = ratio_of(blurred, slabs.at[step], start, n, block, count)
        cells = window([(ref, 0) for ref in [ratio] + ratio_refs + [ratio_up]])
        back = blur(cells, (depth_a, row_a, col_a), spread, mixed, n)
        updated[...] = own_refs[-1][...] * back.reshape(n, ROWS, COLS)

    arrays = below + own + ratios + [ratio_up]
    return call(kernel, "piece", arrays, slabs, ops, [n, n], n)


def shards(
    images, start_estimate, view_order, psf_ranks, depth_taps, row_taps, col_taps, rank_weight
):
    count = lax.axis_size("view")
    parts = len(SIZES)
    starts = [sum(SIZES[i + 1 :]) for i in range(parts)]

    def send(cells, by, skip=()):
        pairs = [(i, (i + by) % count) for i in range(count) if i not in skip]
        return lax.ppermute(cells, "view", pairs)

    above = [send(start_estimate, -1, (0,))]
    ops, slabs = build(
        view_order, psf_ranks, rank_weight, depth_taps, row_taps, col_taps, images
    )
    own = [start_estimate[at : at + n] for at, n in zip(starts, SIZES)]
    first, _ = lax.optimization_barrier((own[:2], ops[0]))
    rest, _ = lax.optimization_barrier((own[2:], above[0]))
    below = [send(piece, 1, (count - 1,)) for piece in list(first) + list(rest)]

    for step in range(STEPS):
        last = step == STEPS - 1
        ratio_up = upper_ratio(step, own[::-1], above, slabs, ops)
        if step > 0:
            lowest, _ = lax.optimization_barrier((own[-1], ratio_up))
            below.append(send(lowest, 1, (step - 1,)))
        ratios, updated, arrived = [], [], []
        for i in range(parts):
            ratio, piece = piece_update(
                step, i, below[i::-1], own[: i - 1 : -1] if i else own[::-1], ratios[::-1],
                ratio_up, slabs, ops,
            )
            ratios.append(ratio)
            updated.append(piece)
            arrived.append(send(piece, 1 - STEPS if last else 1))
        own = arrived
        above = updated[::-1]
        if not last:
            below = [send(piece, 1, (step,)) for piece in own[:-1]]
    return jnp.concatenate(own[::-1], axis=0)


def solution(mesh):
    in_specs = (
        P(("groups", "view"), None, None, None, None),
        P(("groups", "view"), None, None),
        P(),
        P(),
        P(),
        P(),
        P(),
        P(),
    )
    out_specs = P(("groups", "view"), None, None)
    return jax.shard_map(shards, mesh=mesh, in_specs=in_specs, out_specs=out_specs, check_vma=False)
```

```python
import jax
import jax.numpy as jnp
from jax import lax
from jax.experimental import pallas as pl
from jax.experimental.pallas import tpu as pltpu
from jax.sharding import PartitionSpec as P

STEPS = 4
PLANES = 16
MARGIN = 8
SIZES = (8, 8)
ROWS = 64
COLS = 256
GROUP = 8
QUAD = 4
TILE = 256

F32 = jnp.float32
BF16 = jnp.bfloat16
VMEM = pl.BlockSpec(memory_space=pltpu.VMEM)
SMEM = pl.BlockSpec(memory_space=pltpu.SMEM)
COST = pl.CostEstimate(flops=2**20, bytes_accessed=2**10, transcendentals=0)
HBM = pl.BlockSpec(memory_space=pltpu.HBM)


def dot(a, b):
    return jnp.dot(a, b, preferred_element_type=F32)


def iota(shape, dim):
    return lax.broadcasted_iota(jnp.int32, shape, dim)


def build_kernel(
    order, live, weight, depth_taps, row_taps, col_taps, images,
    depth_f, depth_a, row_f, row_a, col_f, col_a, slabs, held, sem,
):
    copy = pltpu.make_async_copy(images.at[0], slabs, sem)
    copy.start()
    views = order.shape[0]
    ranks, count = depth_taps.shape[1:]
    margin = count // 2
    view = order[lax.rem(lax.axis_index("view"), views)]
    square = (TILE, TILE)

    def normal(taps):
        values = taps[view]
        return values / jnp.sum(values, axis=1, keepdims=True)

    rank = iota((ranks, 1), 0)
    weights = jnp.zeros((ranks, 1), F32)
    for r in range(ranks):
        weights = jnp.where(rank == r, weight[view, r], weights)
    weights = jnp.where(rank < live[view], weights, 0.0)
    weights = weights / jnp.sum(weights, axis=0, keepdims=True)

    def placed(values, place):
        held[...] = jnp.zeros(held.shape, F32)
        held[0:ranks, 0:count] = values
        k = iota((held.shape[1], TILE), 0)
        picks = (k < count) & (iota((held.shape[1], TILE), 1) == place(k))
        return dot(held[...].astype(BF16), picks.astype(F32).astype(BF16))

    def rolled(rows, r, n):
        full = jnp.broadcast_to(rows[r : r + 1], (n, TILE))
        return pltpu.roll(full, 0, 1, stride=1, stride_axis=0)

    depth = normal(depth_taps) * weights
    ahead = placed(depth, lambda k: GROUP * k)
    back = placed(depth, lambda k: GROUP * (count - 1 - k))
    for r in range(ranks):
        depth_f[r] = rolled(ahead, r, PLANES * GROUP).astype(BF16)
        depth_a[r] = rolled(back, r, PLANES * GROUP).astype(BF16)

    i, j = iota(square, 0), iota(square, 1)
    near = jnp.abs(j - i) <= margin
    col = normal(col_taps)
    ahead = placed(col, lambda k: (margin - k) & (TILE - 1))
    back = placed(col, lambda k: (k - margin) & (TILE - 1))
    for r in range(ranks):
        col_f[r] = jnp.where(near, rolled(ahead, r, TILE), 0.0).astype(BF16)
        col_a[r] = jnp.where(near, rolled(back, r, TILE), 0.0).astype(BF16)

    near = near & ((i >> 6) == (j >> 6))
    place = ROWS * ((j >> 3) & (QUAD - 1)) + GROUP * (j >> 5) + (j & (GROUP - 1))
    order_columns = (i == place).astype(F32).astype(BF16)
    row = normal(row_taps)
    ahead = placed(row, lambda k: (k - margin) & (TILE - 1))
    back = placed(row, lambda k: (margin - k) & (TILE - 1))
    for r in range(ranks):
        band = jnp.where(near, rolled(ahead, r, TILE), 0.0).astype(BF16)
        row_f[r] = dot(band, order_columns).astype(BF16)
        band = jnp.where(near, rolled(back, r, TILE), 0.0).astype(BF16)
        row_a[r] = dot(band, order_columns).astype(BF16)
    copy.wait()


def build(view_order, psf_ranks, rank_weight, depth_taps, row_taps, col_taps, images):
    ranks = depth_taps.shape[1]
    depth = jax.ShapeDtypeStruct((ranks, PLANES * GROUP, TILE), BF16)
    square = jax.ShapeDtypeStruct((ranks, TILE, TILE), BF16)
    slabs = jax.ShapeDtypeStruct(images.shape[1:], BF16)
    *ops, slabs = pl.pallas_call(
        build_kernel,
        out_shape=[depth, depth] + [square] * 4 + [slabs],
        in_specs=[SMEM] * 3 + [VMEM] * 3 + [HBM],
        out_specs=[VMEM] * 7,
        scratch_shapes=[pltpu.VMEM((8, 128), F32), pltpu.SemaphoreType.DMA],
        compiler_params=pltpu.CompilerParams(vmem_limit_bytes=20 * 2**20),
        name="build",
    )(view_order, psf_ranks, rank_weight, depth_taps, row_taps, col_taps, images)
    return ops, slabs


def blur(cells_of, ops, spread, mixed, planes):
    depth, row, col = ops
    ranks = depth.shape[0]
    lhs = depth[:, 0 : planes * GROUP, :].reshape(ranks * planes * GROUP, TILE)
    for g in range(ROWS // GROUP):
        cells = cells_of(slice(g * GROUP, (g + 1) * GROUP))
        out = dot(lhs, cells.reshape(TILE, COLS).astype(BF16)).astype(BF16)
        out = out.reshape(ranks, planes // QUAD, QUAD * GROUP, COLS)
        spread[:, 0 : planes // QUAD, g * QUAD * GROUP : (g + 1) * QUAD * GROUP, :] = out
    for t in range(planes // QUAD):
        for r in range(ranks):
            mixed[t * TILE : (t + 1) * TILE, r * COLS : (r + 1) * COLS] = dot(
                row[r], spread[r, t]
            ).astype(BF16)
    return dot(mixed[0 : planes * ROWS, :], col[...].reshape(ranks * COLS, COLS))


def window(refs, scales=None):
    def read(y):
        parts, left = [], 2 * PLANES
        for i, (ref, at) in enumerate(refs):
            n = min(left, ref.shape[0] - at)
            cells = ref[at : at + n, y, :]
            if scales is not None and scales[i] is not None:
                cells = cells * scales[i]
            parts.append(cells)
            left -= n
        while left > 0:
            n = min(left, parts[0].shape[0])
            parts.append(parts[0][:n])
            left -= n
        return jnp.concatenate(parts, axis=0)

    return read


def ratio_of(blurred, slab, q, planes, block, count):
    blurred = blurred.reshape(planes, ROWS, COLS)
    z = iota((planes, 1, 1), 0) + (q + block * PLANES - MARGIN)
    inside = (z >= 0) & (z < count * PLANES)
    return jnp.where(inside, slab[q : q + planes].astype(F32), 0.0) / blurred


def block_of(step):
    count = lax.axis_size("view")
    return lax.rem(lax.axis_index("view") + (count - step), count), count


def call(kernel, name, arrays, slabs, ops, outs, planes):
    ranks = ops[0].shape[0]
    out = [jax.ShapeDtypeStruct((n, ROWS, COLS), F32) for n in outs]
    return pl.pallas_call(
        kernel,
        out_shape=out,
        in_specs=[VMEM] * (len(arrays) + 1 + len(ops)),
        out_specs=[VMEM] * len(out),
        scratch_shapes=[
            pltpu.VMEM((ranks, planes // QUAD, TILE, COLS), BF16),
            pltpu.VMEM((planes * ROWS, ranks * COLS), BF16),
        ],
        compiler_params=pltpu.CompilerParams(vmem_limit_bytes=20 * 2**20),
        cost_estimate=COST,
        name=name,
    )(*arrays, slabs, *ops)


def upper_ratio(step, own, above, slabs, ops):
    def kernel(*refs):
        block, count = block_of(step)
        refs = list(refs)
        own_refs = [refs.pop(0) for _ in own]
        above_refs = [refs.pop(0) for _ in above]
        slabs, depth, row, col, ratio, spread, mixed = refs
        scale = (block < count - 1).astype(F32)
        scales = [None] * len(own) + [scale] * len(above)
        cells = window([(ref, 0) for ref in own_refs + above_refs], scales)
        blurred = blur(cells, (depth, row, col), spread, mixed, PLANES)
        ratio[...] = ratio_of(blurred, slabs.at[step], PLANES, PLANES, block, count)

    arrays = own + above
    return call(kernel, "upper", arrays, slabs, ops[0::2], [PLANES], PLANES)[0]


def piece_update(step, index, below, own, ratios, ratio_up, slabs, ops):
    n = own[-1].shape[0]
    start = sum(SIZES[index + 1 :])

    def kernel(*refs):
        block, count = block_of(step)
        refs = list(refs)
        below_refs = [refs.pop(0) for _ in below]
        own_refs = [refs.pop(0) for _ in own]
        ratio_refs = [refs.pop(0) for _ in ratios]
        ratio_up, slabs = refs[:2]
        depth_f, depth_a, row_f, row_a, col_f, col_a = refs[2:8]
        ratio, updated, spread, mixed = refs[8:]
        cells = window([(ref, 0) for ref in below_refs + own_refs])
        blurred = blur(cells, (depth_f, row_f, col_f), spread, mixed, n)
        ratio[...] = ratio_of(blurred, slabs.at[step], start, n, block, count)
        cells = window([(ref, 0) for ref in [ratio] + ratio_refs + [ratio_up]])
        back = blur(cells, (depth_a, row_a, col_a), spread, mixed, n)
        updated[...] = own_refs[-1][...] * back.reshape(n, ROWS, COLS)

    arrays = below + own + ratios + [ratio_up]
    return call(kernel, "piece", arrays, slabs, ops, [n, n], n)


def shards(
    images, start_estimate, view_order, psf_ranks, depth_taps, row_taps, col_taps, rank_weight
):
    count = lax.axis_size("view")
    parts = len(SIZES)
    starts = [sum(SIZES[i + 1 :]) for i in range(parts)]

    def send(cells, by, skip=()):
        pairs = [(i, (i + by) % count) for i in range(count) if i not in skip]
        return lax.ppermute(cells, "view", pairs)

    above = [send(start_estimate, -1, (0,))]
    ops, slabs = build(
        view_order, psf_ranks, rank_weight, depth_taps, row_taps, col_taps, images
    )
    own = [start_estimate[at : at + n] for at, n in zip(starts, SIZES)]
    later, _ = lax.optimization_barrier((own, ops[0]))
    below = [send(piece, 1, (count - 1,)) for piece in later]

    for step in range(STEPS):
        last = step == STEPS - 1
        ratio_up = upper_ratio(step, own[::-1], above, slabs, ops)
        ratios, updated, arrived = [], [], []
        for i in range(parts):
            ratio, piece = piece_update(
                step, i, below[i::-1], own[: i - 1 : -1] if i else own[::-1], ratios[::-1],
                ratio_up, slabs, ops,
            )
            ratios.append(ratio)
            updated.append(piece)
            arrived.append(send(piece, 1 - STEPS if last else 1))
        own = arrived
        above = updated[::-1]
        if not last:
            below = [send(piece, 1, (step,)) for piece in own]
    return jnp.concatenate(own[::-1], axis=0)


def solution(mesh):
    in_specs = (
        P(("groups", "view"), None, None, None, None),
        P(("groups", "view"), None, None),
        P(),
        P(),
        P(),
        P(),
        P(),
        P(),
    )
    out_specs = P(("groups", "view"), None, None)
    return jax.shard_map(shards, mesh=mesh, in_specs=in_specs, out_specs=out_specs, check_vma=False)
```

```python
import jax
import jax.numpy as jnp
from jax import lax
from jax.experimental import pallas as pl
from jax.experimental.pallas import tpu as pltpu
from jax.sharding import PartitionSpec as P

STEPS = 4
PLANES = 16
MARGIN = 8
HALF = 8
ROWS = 64
COLS = 256
GROUP = 8
QUAD = 4
TILE = 256

F32 = jnp.float32
BF16 = jnp.bfloat16
VMEM = pl.BlockSpec(memory_space=pltpu.VMEM)
SMEM = pl.BlockSpec(memory_space=pltpu.SMEM)
COST = pl.CostEstimate(flops=2**20, bytes_accessed=2**10, transcendentals=0)
HBM = pl.BlockSpec(memory_space=pltpu.HBM)


def dot(a, b):
    return jnp.dot(a, b, preferred_element_type=F32)


def iota(shape, dim):
    return lax.broadcasted_iota(jnp.int32, shape, dim)


def build_kernel(
    order, live, weight, depth_taps, row_taps, col_taps, images,
    depth_f, depth_a, row_f, row_a, col_f, col_a, slabs, held, sem,
):
    copy = pltpu.make_async_copy(images.at[0], slabs, sem)
    copy.start()
    views = order.shape[0]
    ranks, count = depth_taps.shape[1:]
    margin = count // 2
    view = order[lax.rem(lax.axis_index("view"), views)]
    square = (TILE, TILE)

    def normal(taps):
        values = taps[view]
        return values / jnp.sum(values, axis=1, keepdims=True)

    rank = iota((ranks, 1), 0)
    weights = jnp.zeros((ranks, 1), F32)
    for r in range(ranks):
        weights = jnp.where(rank == r, weight[view, r], weights)
    weights = jnp.where(rank < live[view], weights, 0.0)
    weights = weights / jnp.sum(weights, axis=0, keepdims=True)

    def placed(values, place):
        held[...] = jnp.zeros(held.shape, F32)
        held[0:ranks, 0:count] = values
        k = iota((held.shape[1], TILE), 0)
        picks = (k < count) & (iota((held.shape[1], TILE), 1) == place(k))
        return dot(held[...].astype(BF16), picks.astype(F32).astype(BF16))

    def rolled(rows, r, n):
        full = jnp.broadcast_to(rows[r : r + 1], (n, TILE))
        return pltpu.roll(full, 0, 1, stride=1, stride_axis=0)

    depth = normal(depth_taps) * weights
    ahead = placed(depth, lambda k: GROUP * k)
    back = placed(depth, lambda k: GROUP * (count - 1 - k))
    for r in range(ranks):
        depth_f[r] = rolled(ahead, r, PLANES * GROUP).astype(BF16)
        depth_a[r] = rolled(back, r, PLANES * GROUP).astype(BF16)

    i, j = iota(square, 0), iota(square, 1)
    near = jnp.abs(j - i) <= margin
    col = normal(col_taps)
    ahead = placed(col, lambda k: (margin - k) & (TILE - 1))
    back = placed(col, lambda k: (k - margin) & (TILE - 1))
    for r in range(ranks):
        col_f[r] = jnp.where(near, rolled(ahead, r, TILE), 0.0).astype(BF16)
        col_a[r] = jnp.where(near, rolled(back, r, TILE), 0.0).astype(BF16)

    near = near & ((i >> 6) == (j >> 6))
    place = ROWS * ((j >> 3) & (QUAD - 1)) + GROUP * (j >> 5) + (j & (GROUP - 1))
    order_columns = (i == place).astype(F32).astype(BF16)
    row = normal(row_taps)
    ahead = placed(row, lambda k: (k - margin) & (TILE - 1))
    back = placed(row, lambda k: (margin - k) & (TILE - 1))
    for r in range(ranks):
        band = jnp.where(near, rolled(ahead, r, TILE), 0.0).astype(BF16)
        row_f[r] = dot(band, order_columns).astype(BF16)
        band = jnp.where(near, rolled(back, r, TILE), 0.0).astype(BF16)
        row_a[r] = dot(band, order_columns).astype(BF16)
    copy.wait()


def build(view_order, psf_ranks, rank_weight, depth_taps, row_taps, col_taps, images):
    ranks = depth_taps.shape[1]
    depth = jax.ShapeDtypeStruct((ranks, PLANES * GROUP, TILE), BF16)
    square = jax.ShapeDtypeStruct((ranks, TILE, TILE), BF16)
    slabs = jax.ShapeDtypeStruct(images.shape[1:], BF16)
    *ops, slabs = pl.pallas_call(
        build_kernel,
        out_shape=[depth, depth] + [square] * 4 + [slabs],
        in_specs=[SMEM] * 3 + [VMEM] * 3 + [HBM],
        out_specs=[VMEM] * 7,
        scratch_shapes=[pltpu.VMEM((8, 128), F32), pltpu.SemaphoreType.DMA],
        compiler_params=pltpu.CompilerParams(vmem_limit_bytes=20 * 2**20),
        name="build",
    )(view_order, psf_ranks, rank_weight, depth_taps, row_taps, col_taps, images)
    return ops, slabs


def blur(cells_of, ops, spread, mixed, planes):
    depth, row, col = ops
    ranks = depth.shape[0]
    lhs = depth[:, 0 : planes * GROUP, :].reshape(ranks * planes * GROUP, TILE)
    for g in range(ROWS // GROUP):
        cells = cells_of(slice(g * GROUP, (g + 1) * GROUP))
        out = dot(lhs, cells.reshape(TILE, COLS).astype(BF16)).astype(BF16)
        out = out.reshape(ranks, planes // QUAD, QUAD * GROUP, COLS)
        spread[:, 0 : planes // QUAD, g * QUAD * GROUP : (g + 1) * QUAD * GROUP, :] = out
    for t in range(planes // QUAD):
        for r in range(ranks):
            mixed[t * TILE : (t + 1) * TILE, r * COLS : (r + 1) * COLS] = dot(
                row[r], spread[r, t]
            ).astype(BF16)
    return dot(mixed[0 : planes * ROWS, :], col[...].reshape(ranks * COLS, COLS))


def window(refs, scales=None):
    def read(y):
        parts, left = [], 2 * PLANES
        for i, (ref, at) in enumerate(refs):
            n = min(left, ref.shape[0] - at)
            cells = ref[at : at + n, y, :]
            if scales is not None and scales[i] is not None:
                cells = cells * scales[i]
            parts.append(cells)
            left -= n
        while left > 0:
            n = min(left, parts[0].shape[0])
            parts.append(parts[0][:n])
            left -= n
        return jnp.concatenate(parts, axis=0)

    return read


def ratio_of(blurred, slab, q, planes, block, count):
    blurred = blurred.reshape(planes, ROWS, COLS)
    z = iota((planes, 1, 1), 0) + (q + block * PLANES - MARGIN)
    inside = (z >= 0) & (z < count * PLANES)
    return jnp.where(inside, slab[q : q + planes].astype(F32), 0.0) / blurred


def block_of(step):
    count = lax.axis_size("view")
    return lax.rem(lax.axis_index("view") + (count - step), count), count


def by_parity(which, body):
    odd = lax.rem(lax.axis_index("view"), 2)
    for parity in which:
        pl.when(odd == parity)(lambda parity=parity: body(parity))


def call(kernel, name, arrays, slabs, ops, outs, planes):
    ranks = ops[0].shape[0]
    out = [jax.ShapeDtypeStruct((n, ROWS, COLS), F32) for n in outs]
    return pl.pallas_call(
        kernel,
        out_shape=out,
        in_specs=[VMEM] * (len(arrays) + 1 + len(ops)),
        out_specs=[VMEM] * len(out),
        scratch_shapes=[
            pltpu.VMEM((ranks, planes // QUAD, TILE, COLS), BF16),
            pltpu.VMEM((planes * ROWS, ranks * COLS), BF16),
        ],
        compiler_params=pltpu.CompilerParams(vmem_limit_bytes=20 * 2**20),
        cost_estimate=COST,
        name=name,
    )(*arrays, slabs, *ops)


class Operands:
    def __init__(self, *entries):
        self.entries = entries
        self.arrays = []
        for entry in entries:
            for array in entry if isinstance(entry, tuple) else (entry,):
                if not any(array is other for other in self.arrays):
                    self.arrays.append(array)

    def pick(self, refs, parity):
        chosen = [e[parity] if isinstance(e, tuple) else e for e in self.entries]
        return [
            refs[next(i for i, other in enumerate(self.arrays) if other is array)]
            for array in chosen
        ]


def upper_ratio(step, own, above, slabs, ops):
    operands = Operands(*own, *above)
    count_in = len(operands.arrays)

    def kernel(*refs):
        block, count = block_of(step)
        slabs, depth, row, col, ratio, spread, mixed = refs[count_in:]
        scale = (block < count - 1).astype(F32)
        scales = [None] * len(own) + [scale] * len(above)

        def body(parity):
            cells = window([(ref, 0) for ref in operands.pick(refs, parity)], scales)
            blurred = blur(cells, (depth, row, col), spread, mixed, PLANES)
            ratio[...] = ratio_of(blurred, slabs.at[step], PLANES, PLANES, block, count)

        split = any(isinstance(e, tuple) for e in operands.entries)
        by_parity((0, 1), body) if split else body(0)

    return call(kernel, "upper", operands.arrays, slabs, ops[0::2], [PLANES], PLANES)[0]


def half_update(step, which, start, below, own, ratios, slabs, ops):
    operands = Operands(*below, *own, *ratios)
    count_in = len(operands.arrays)
    n = HALF

    def kernel(*refs):
        block, count = block_of(step)
        slabs, depth_f, depth_a, row_f, row_a, col_f, col_a = refs[count_in : count_in + 7]
        ratio, updated, spread, mixed = refs[count_in + 7 :]

        def body(parity):
            chosen = operands.pick(refs, parity)
            blurred_refs = chosen[: len(below) + len(own)]
            cells = window([(ref, 0) for ref in blurred_refs])
            blurred = blur(cells, (depth_f, row_f, col_f), spread, mixed, n)
            ratio[...] = ratio_of(blurred, slabs.at[step], start, n, block, count)
            cells = window([(ref, 0) for ref in [ratio] + chosen[len(below) + len(own) :]])
            back = blur(cells, (depth_a, row_a, col_a), spread, mixed, n)
            updated[...] = blurred_refs[-1][...] * back.reshape(n, ROWS, COLS)

        by_parity(which, body)

    return call(kernel, "half", operands.arrays, slabs, ops, [n, n], n)


def placed_half(pair, start, whole=None):
    pair = pair if isinstance(pair, tuple) else (pair, pair)
    arrays = list(pair) if pair[0] is not pair[1] else [pair[0]]
    extra = [] if whole is None else [whole]

    def kernel(*refs):
        out, sem = refs[-2:]

        def body(parity):
            source = refs[parity if len(arrays) == 2 else 0]
            copy = pltpu.make_async_copy(source, out.at[pl.ds(start, HALF)], sem)
            copy.start()
            copy.wait()

        by_parity((0, 1), body) if len(arrays) == 2 else body(0)

    return pl.pallas_call(
        kernel,
        out_shape=jax.ShapeDtypeStruct((PLANES, ROWS, COLS), F32),
        in_specs=[VMEM] * len(arrays) + [HBM] * len(extra),
        out_specs=HBM,
        scratch_shapes=[pltpu.SemaphoreType.DMA],
        input_output_aliases={len(arrays): 0} if extra else {},
        compiler_params=pltpu.CompilerParams(vmem_limit_bytes=20 * 2**20),
        cost_estimate=COST,
        name="place",
    )(*arrays, *extra)


def shards(
    images, start_estimate, view_order, psf_ranks, depth_taps, row_taps, col_taps, rank_weight
):
    count = lax.axis_size("view")

    def send(cells, by, skip=(), parities=(0, 1)):
        pairs = [
            (i, (i + by) % count) for i in range(count) if i not in skip and i % 2 in parities
        ]
        return lax.ppermute(cells, "view", pairs)

    above = [send(start_estimate, -1, (0,))]
    ops, slabs = build(
        view_order, psf_ranks, rank_weight, depth_taps, row_taps, col_taps, images
    )
    own_lo, own_hi = start_estimate[:HALF], start_estimate[HALF:]
    (early_hi, early_lo), _ = lax.optimization_barrier(((own_hi, own_lo), ops[0]))
    below_hi = send(early_hi, 1, (count - 1,))
    below_lo = send(early_lo, 1, (count - 1,))

    for step in range(STEPS):
        last = step == STEPS - 1
        by = 1 - STEPS if last else 1
        ratio_up = upper_ratio(step, [own_lo, own_hi], above, slabs, ops)
        below = below_hi if isinstance(below_hi, tuple) else (below_hi, below_hi)
        own = own_hi if isinstance(own_hi, tuple) else (own_hi, own_hi)
        ratio_odd, odd_hi = half_update(
            step, (1,), HALF, [below[1]], [own_lo, own[1]], [ratio_up], slabs, ops
        )
        from_odd = send(odd_hi, by, (), (1,))
        ratio_up_later, _ = lax.optimization_barrier((ratio_up, odd_hi))
        ratio_even, even_hi = half_update(
            step, (0,), HALF, [below[0]], [own_lo, own[0]], [ratio_up_later], slabs, ops
        )
        from_even = send(even_hi, by, (), (0,))
        ratio_mid = (ratio_even, ratio_odd)
        _, lo = half_update(
            step, (0, 1), 0, [below_lo, below_hi], [own_lo], [ratio_mid, ratio_up_later], slabs, ops
        )
        above = [lo, (even_hi, odd_hi)]
        own_hi = (from_odd, from_even)
        own_lo = send(lo, by)
        if not last:
            to_odd = send(from_odd, 1, (step,), (0,))
            later, _ = lax.optimization_barrier((from_even, from_odd))
            to_even = send(later, 1, (step,), (1,))
            below_hi = (to_even, to_odd)
            below_lo = send(own_lo, 1, (step,))
    return placed_half(own_lo, 0, placed_half(own_hi, HALF))


def solution(mesh):
    in_specs = (
        P(("groups", "view"), None, None, None, None),
        P(("groups", "view"), None, None),
        P(),
        P(),
        P(),
        P(),
        P(),
        P(),
    )
    out_specs = P(("groups", "view"), None, None)
    return jax.shard_map(shards, mesh=mesh, in_specs=in_specs, out_specs=out_specs, check_vma=False)
```

```python
import jax
import jax.numpy as jnp
from jax import lax
from jax.experimental import pallas as pl
from jax.experimental.pallas import tpu as pltpu
from jax.sharding import PartitionSpec as P

STEPS = 4
PLANES = 16
MARGIN = 8
HALF = 8
ROWS = 64
COLS = 256
GROUP = 8
QUAD = 4
TILE = 256

F32 = jnp.float32
BF16 = jnp.bfloat16
VMEM = pl.BlockSpec(memory_space=pltpu.VMEM)
SMEM = pl.BlockSpec(memory_space=pltpu.SMEM)
COST = pl.CostEstimate(flops=2**20, bytes_accessed=2**10, transcendentals=0)
HBM = pl.BlockSpec(memory_space=pltpu.HBM)


def dot(a, b):
    return jnp.dot(a, b, preferred_element_type=F32)


def iota(shape, dim):
    return lax.broadcasted_iota(jnp.int32, shape, dim)


def build_kernel(
    order, live, weight, depth_taps, row_taps, col_taps, images,
    depth_f, depth_a, row_f, row_a, col_f, col_a, slabs, held, sem,
):
    copy = pltpu.make_async_copy(images.at[0], slabs, sem)
    copy.start()
    views = order.shape[0]
    ranks, count = depth_taps.shape[1:]
    margin = count // 2
    view = order[lax.rem(lax.axis_index("view"), views)]
    square = (TILE, TILE)

    def normal(taps):
        values = taps[view]
        return values / jnp.sum(values, axis=1, keepdims=True)

    rank = iota((ranks, 1), 0)
    weights = jnp.zeros((ranks, 1), F32)
    for r in range(ranks):
        weights = jnp.where(rank == r, weight[view, r], weights)
    weights = jnp.where(rank < live[view], weights, 0.0)
    weights = weights / jnp.sum(weights, axis=0, keepdims=True)

    def placed(values, place):
        held[...] = jnp.zeros(held.shape, F32)
        held[0:ranks, 0:count] = values
        k = iota((held.shape[1], TILE), 0)
        picks = (k < count) & (iota((held.shape[1], TILE), 1) == place(k))
        return dot(held[...].astype(BF16), picks.astype(F32).astype(BF16))

    def rolled(rows, r, n):
        full = jnp.broadcast_to(rows[r : r + 1], (n, TILE))
        return pltpu.roll(full, 0, 1, stride=1, stride_axis=0)

    depth = normal(depth_taps) * weights
    ahead = placed(depth, lambda k: GROUP * k)
    back = placed(depth, lambda k: GROUP * (count - 1 - k))
    for r in range(ranks):
        depth_f[r] = rolled(ahead, r, PLANES * GROUP).astype(BF16)
        depth_a[r] = rolled(back, r, PLANES * GROUP).astype(BF16)

    i, j = iota(square, 0), iota(square, 1)
    near = jnp.abs(j - i) <= margin
    col = normal(col_taps)
    ahead = placed(col, lambda k: (margin - k) & (TILE - 1))
    back = placed(col, lambda k: (k - margin) & (TILE - 1))
    for r in range(ranks):
        col_f[r] = jnp.where(near, rolled(ahead, r, TILE), 0.0).astype(BF16)
        col_a[r] = jnp.where(near, rolled(back, r, TILE), 0.0).astype(BF16)

    near = near & ((i >> 6) == (j >> 6))
    place = ROWS * ((j >> 3) & (QUAD - 1)) + GROUP * (j >> 5) + (j & (GROUP - 1))
    order_columns = (i == place).astype(F32).astype(BF16)
    row = normal(row_taps)
    ahead = placed(row, lambda k: (k - margin) & (TILE - 1))
    back = placed(row, lambda k: (margin - k) & (TILE - 1))
    for r in range(ranks):
        band = jnp.where(near, rolled(ahead, r, TILE), 0.0).astype(BF16)
        row_f[r] = dot(band, order_columns).astype(BF16)
        band = jnp.where(near, rolled(back, r, TILE), 0.0).astype(BF16)
        row_a[r] = dot(band, order_columns).astype(BF16)
    copy.wait()


def build(view_order, psf_ranks, rank_weight, depth_taps, row_taps, col_taps, images):
    ranks = depth_taps.shape[1]
    depth = jax.ShapeDtypeStruct((ranks, PLANES * GROUP, TILE), BF16)
    square = jax.ShapeDtypeStruct((ranks, TILE, TILE), BF16)
    slabs = jax.ShapeDtypeStruct(images.shape[1:], BF16)
    *ops, slabs = pl.pallas_call(
        build_kernel,
        out_shape=[depth, depth] + [square] * 4 + [slabs],
        in_specs=[SMEM] * 3 + [VMEM] * 3 + [HBM],
        out_specs=[VMEM] * 7,
        scratch_shapes=[pltpu.VMEM((8, 128), F32), pltpu.SemaphoreType.DMA],
        compiler_params=pltpu.CompilerParams(vmem_limit_bytes=20 * 2**20),
        name="build",
    )(view_order, psf_ranks, rank_weight, depth_taps, row_taps, col_taps, images)
    return ops, slabs


def blur(cells_of, ops, spread, mixed, planes):
    depth, row, col = ops
    ranks = depth.shape[0]
    lhs = depth[:, 0 : planes * GROUP, :].reshape(ranks * planes * GROUP, TILE)
    for g in range(ROWS // GROUP):
        cells = cells_of(slice(g * GROUP, (g + 1) * GROUP))
        out = dot(lhs, cells.reshape(TILE, COLS).astype(BF16)).astype(BF16)
        out = out.reshape(ranks, planes // QUAD, QUAD * GROUP, COLS)
        spread[:, 0 : planes // QUAD, g * QUAD * GROUP : (g + 1) * QUAD * GROUP, :] = out
    for t in range(planes // QUAD):
        for r in range(ranks):
            mixed[t * TILE : (t + 1) * TILE, r * COLS : (r + 1) * COLS] = dot(
                row[r], spread[r, t]
            ).astype(BF16)
    return dot(mixed[0 : planes * ROWS, :], col[...].reshape(ranks * COLS, COLS))


def window(refs, scales=None):
    def read(y):
        parts, left = [], 2 * PLANES
        for i, (ref, at) in enumerate(refs):
            n = min(left, ref.shape[0] - at)
            cells = ref[at : at + n, y, :]
            if scales is not None and scales[i] is not None:
                cells = cells * scales[i]
            parts.append(cells)
            left -= n
        while left > 0:
            n = min(left, parts[0].shape[0])
            parts.append(parts[0][:n])
            left -= n
        return jnp.concatenate(parts, axis=0)

    return read


def ratio_of(blurred, slab, q, planes, block, count):
    blurred = blurred.reshape(planes, ROWS, COLS)
    z = iota((planes, 1, 1), 0) + (q + block * PLANES - MARGIN)
    inside = (z >= 0) & (z < count * PLANES)
    return jnp.where(inside, slab[q : q + planes].astype(F32), 0.0) / blurred


def block_of(step):
    count = lax.axis_size("view")
    return lax.rem(lax.axis_index("view") + (count - step), count), count


def by_parity(which, body):
    odd = lax.rem(lax.axis_index("view"), 2)
    for parity in which:
        pl.when(odd == parity)(lambda parity=parity: body(parity))


def call(kernel, name, arrays, slabs, ops, outs, planes):
    ranks = ops[0].shape[0]
    out = [jax.ShapeDtypeStruct((n, ROWS, COLS), F32) for n in outs]
    return pl.pallas_call(
        kernel,
        out_shape=out,
        in_specs=[VMEM] * (len(arrays) + 1 + len(ops)),
        out_specs=[VMEM] * len(out),
        scratch_shapes=[
            pltpu.VMEM((ranks, planes // QUAD, TILE, COLS), BF16),
            pltpu.VMEM((planes * ROWS, ranks * COLS), BF16),
        ],
        compiler_params=pltpu.CompilerParams(vmem_limit_bytes=20 * 2**20),
        cost_estimate=COST,
        name=name,
    )(*arrays, slabs, *ops)


class Operands:
    def __init__(self, *entries):
        self.entries = entries
        self.arrays = []
        for entry in entries:
            for array in entry if isinstance(entry, tuple) else (entry,):
                if not any(array is other for other in self.arrays):
                    self.arrays.append(array)

    def pick(self, refs, parity):
        chosen = [e[parity] if isinstance(e, tuple) else e for e in self.entries]
        return [
            refs[next(i for i, other in enumerate(self.arrays) if other is array)]
            for array in chosen
        ]


def upper_ratio(step, own, above, slabs, ops):
    operands = Operands(*own, *above)
    count_in = len(operands.arrays)

    def kernel(*refs):
        block, count = block_of(step)
        slabs, depth, row, col, ratio, spread, mixed = refs[count_in:]
        scale = (block < count - 1).astype(F32)
        scales = [None] * len(own) + [scale] * len(above)

        def body(parity):
            cells = window([(ref, 0) for ref in operands.pick(refs, parity)], scales)
            blurred = blur(cells, (depth, row, col), spread, mixed, PLANES)
            ratio[...] = ratio_of(blurred, slabs.at[step], PLANES, PLANES, block, count)

        split = any(isinstance(e, tuple) for e in operands.entries)
        by_parity((0, 1), body) if split else body(0)

    return call(kernel, "upper", operands.arrays, slabs, ops[0::2], [PLANES], PLANES)[0]


def half_update(step, which, start, below, own, ratios, slabs, ops):
    operands = Operands(*below, *own, *ratios)
    count_in = len(operands.arrays)
    n = HALF

    def kernel(*refs):
        block, count = block_of(step)
        slabs, depth_f, depth_a, row_f, row_a, col_f, col_a = refs[count_in : count_in + 7]
        ratio, updated, spread, mixed = refs[count_in + 7 :]

        scale = (block > 0).astype(F32)
        scales = [scale] * len(below) + [None] * len(own)

        def body(parity):
            chosen = operands.pick(refs, parity)
            blurred_refs = chosen[: len(below) + len(own)]
            cells = window([(ref, 0) for ref in blurred_refs], scales)
            blurred = blur(cells, (depth_f, row_f, col_f), spread, mixed, n)
            ratio[...] = ratio_of(blurred, slabs.at[step], start, n, block, count)
            cells = window([(ref, 0) for ref in [ratio] + chosen[len(below) + len(own) :]])
            back = blur(cells, (depth_a, row_a, col_a), spread, mixed, n)
            updated[...] = blurred_refs[-1][...] * back.reshape(n, ROWS, COLS)

        split = len(which) < 2 or any(isinstance(e, tuple) for e in operands.entries)
        by_parity(which, body) if split else body(0)

    return call(kernel, "half", operands.arrays, slabs, ops, [n, n], n)


def placed_half(pair, start, whole=None):
    pair = pair if isinstance(pair, tuple) else (pair, pair)
    arrays = list(pair) if pair[0] is not pair[1] else [pair[0]]
    extra = [] if whole is None else [whole]

    def kernel(*refs):
        out, sem = refs[-2:]

        def body(parity):
            source = refs[parity if len(arrays) == 2 else 0]
            copy = pltpu.make_async_copy(source, out.at[pl.ds(start, HALF)], sem)
            copy.start()
            copy.wait()

        by_parity((0, 1), body) if len(arrays) == 2 else body(0)

    return pl.pallas_call(
        kernel,
        out_shape=jax.ShapeDtypeStruct((PLANES, ROWS, COLS), F32),
        in_specs=[VMEM] * len(arrays) + [HBM] * len(extra),
        out_specs=HBM,
        scratch_shapes=[pltpu.SemaphoreType.DMA],
        input_output_aliases={len(arrays): 0} if extra else {},
        compiler_params=pltpu.CompilerParams(vmem_limit_bytes=20 * 2**20),
        cost_estimate=COST,
        name="place",
    )(*arrays, *extra)


def shards(
    images, start_estimate, view_order, psf_ranks, depth_taps, row_taps, col_taps, rank_weight
):
    count = lax.axis_size("view")

    def send(cells, by):
        return lax.ppermute(cells, "view", [(i, (i + by) % count) for i in range(count)])

    above = [send(start_estimate, -1)]
    ops, slabs = build(
        view_order, psf_ranks, rank_weight, depth_taps, row_taps, col_taps, images
    )
    own_lo, own_hi = start_estimate[:HALF], start_estimate[HALF:]
    (early_hi, early_lo), _ = lax.optimization_barrier(((own_hi, own_lo), ops[0]))
    below_hi = send(early_hi, 1)
    below_lo = send(early_lo, 1)

    for step in range(STEPS):
        last = step == STEPS - 1
        by = 1 - STEPS if last else 1
        ratio_up = upper_ratio(step, [own_lo, own_hi], above, slabs, ops)
        ratio_mid, hi = half_update(
            step, (0, 1), HALF, [below_hi], [own_lo, own_hi], [ratio_up], slabs, ops
        )
        next_hi = send(hi, by)
        _, lo = half_update(
            step, (0, 1), 0, [below_lo, below_hi], [own_lo], [ratio_mid, ratio_up], slabs, ops
        )
        above = [lo, hi]
        own_lo, own_hi = send(lo, by), next_hi
        if not last:
            below_hi = send(own_hi, 1)
            below_lo = send(own_lo, 1)
    return placed_half(own_lo, 0, placed_half(own_hi, HALF))


def solution(mesh):
    in_specs = (
        P(("groups", "view"), None, None, None, None),
        P(("groups", "view"), None, None),
        P(),
        P(),
        P(),
        P(),
        P(),
        P(),
    )
    out_specs = P(("groups", "view"), None, None)
    return jax.shard_map(shards, mesh=mesh, in_specs=in_specs, out_specs=out_specs, check_vma=False)
```

```python
import jax
import jax.numpy as jnp
from jax import lax
from jax.experimental import pallas as pl
from jax.experimental.pallas import tpu as pltpu
from jax.sharding import PartitionSpec as P

STEPS = 4
PLANES = 16
MARGIN = 8
HALF = 8
ROWS = 64
COLS = 256
GROUP = 8
QUAD = 4
TILE = 256

F32 = jnp.float32
BF16 = jnp.bfloat16
VMEM = pl.BlockSpec(memory_space=pltpu.VMEM)
SMEM = pl.BlockSpec(memory_space=pltpu.SMEM)
COST = pl.CostEstimate(flops=2**20, bytes_accessed=2**10, transcendentals=0)
HBM = pl.BlockSpec(memory_space=pltpu.HBM)


def dot(a, b):
    return jnp.dot(a, b, preferred_element_type=F32)


def iota(shape, dim):
    return lax.broadcasted_iota(jnp.int32, shape, dim)


def build_kernel(
    place, order, live, weight, depth_taps, row_taps, col_taps, images,
    depth_f, depth_a, row_f, row_a, col_f, col_a, slabs, ends, held, sem,
):
    copy = pltpu.make_async_copy(images.at[0], slabs, sem)
    copy.start()
    position, devices = place[0], place[1]
    for step in range(STEPS):
        block = lax.rem(position + (devices - step), devices)
        ends[step] = jnp.full((1, COLS), (block > 0).astype(F32))
        ends[STEPS + step] = jnp.full((1, COLS), (block < devices - 1).astype(F32))
    views = order.shape[0]
    ranks, count = depth_taps.shape[1:]
    margin = count // 2
    view = order[lax.rem(position, views)]
    square = (TILE, TILE)

    def normal(taps):
        values = taps[view]
        return values / jnp.sum(values, axis=1, keepdims=True)

    rank = iota((ranks, 1), 0)
    weights = jnp.zeros((ranks, 1), F32)
    for r in range(ranks):
        weights = jnp.where(rank == r, weight[view, r], weights)
    weights = jnp.where(rank < live[view], weights, 0.0)
    weights = weights / jnp.sum(weights, axis=0, keepdims=True)

    def placed(values, place):
        held[...] = jnp.zeros(held.shape, F32)
        held[0:ranks, 0:count] = values
        k = iota((held.shape[1], TILE), 0)
        picks = (k < count) & (iota((held.shape[1], TILE), 1) == place(k))
        return dot(held[...].astype(BF16), picks.astype(F32).astype(BF16))

    def rolled(rows, r, n):
        full = jnp.broadcast_to(rows[r : r + 1], (n, TILE))
        return pltpu.roll(full, 0, 1, stride=1, stride_axis=0)

    depth = normal(depth_taps) * weights
    ahead = placed(depth, lambda k: GROUP * k)
    back = placed(depth, lambda k: GROUP * (count - 1 - k))
    for r in range(ranks):
        depth_f[r] = rolled(ahead, r, PLANES * GROUP).astype(BF16)
        depth_a[r] = rolled(back, r, PLANES * GROUP).astype(BF16)

    i, j = iota(square, 0), iota(square, 1)
    near = jnp.abs(j - i) <= margin
    col = normal(col_taps)
    ahead = placed(col, lambda k: (margin - k) & (TILE - 1))
    back = placed(col, lambda k: (k - margin) & (TILE - 1))
    for r in range(ranks):
        col_f[r] = jnp.where(near, rolled(ahead, r, TILE), 0.0).astype(BF16)
        col_a[r] = jnp.where(near, rolled(back, r, TILE), 0.0).astype(BF16)

    near = near & ((i >> 6) == (j >> 6))
    place = ROWS * ((j >> 3) & (QUAD - 1)) + GROUP * (j >> 5) + (j & (GROUP - 1))
    order_columns = (i == place).astype(F32).astype(BF16)
    row = normal(row_taps)
    ahead = placed(row, lambda k: (k - margin) & (TILE - 1))
    back = placed(row, lambda k: (margin - k) & (TILE - 1))
    for r in range(ranks):
        band = jnp.where(near, rolled(ahead, r, TILE), 0.0).astype(BF16)
        row_f[r] = dot(band, order_columns).astype(BF16)
        band = jnp.where(near, rolled(back, r, TILE), 0.0).astype(BF16)
        row_a[r] = dot(band, order_columns).astype(BF16)
    copy.wait()


def build(place, view_order, psf_ranks, rank_weight, depth_taps, row_taps, col_taps, images):
    ranks = depth_taps.shape[1]
    depth = jax.ShapeDtypeStruct((ranks, PLANES * GROUP, TILE), BF16)
    square = jax.ShapeDtypeStruct((ranks, TILE, TILE), BF16)
    slabs = jax.ShapeDtypeStruct(images.shape[1:], BF16)
    ends = jax.ShapeDtypeStruct((2 * STEPS, 1, COLS), F32)
    *ops, slabs, ends = pl.pallas_call(
        build_kernel,
        out_shape=[depth, depth] + [square] * 4 + [slabs, ends],
        in_specs=[SMEM] * 4 + [VMEM] * 3 + [HBM],
        out_specs=[VMEM] * 8,
        scratch_shapes=[pltpu.VMEM((8, 128), F32), pltpu.SemaphoreType.DMA],
        compiler_params=pltpu.CompilerParams(vmem_limit_bytes=20 * 2**20),
        name="build",
    )(place, view_order, psf_ranks, rank_weight, depth_taps, row_taps, col_taps, images)
    return ops, slabs, ends


def depth_pass(cells_of, op, planes, spread):
    ranks = op.shape[0]
    lhs = op[:, 0 : planes * GROUP, :].reshape(ranks * planes * GROUP, TILE)
    for g in range(ROWS // GROUP):
        cells = cells_of(slice(g * GROUP, (g + 1) * GROUP))
        out = dot(lhs, cells.reshape(TILE, COLS).astype(BF16)).astype(BF16)
        out = out.reshape(ranks, planes // QUAD, QUAD * GROUP, COLS)
        spread[:, :, g * QUAD * GROUP : (g + 1) * QUAD * GROUP, :] = out


def row_pass(spread, op, mixed, t):
    for r in range(op.shape[0]):
        mixed[t * TILE : (t + 1) * TILE, r * COLS : (r + 1) * COLS] = dot(
            op[r], spread[r, t]
        ).astype(BF16)


def col_pass(mixed, op, first, last):
    ranks = op.shape[0]
    out = dot(mixed[first * TILE : last * TILE, :], op[...].reshape(ranks * COLS, COLS))
    return out.reshape((last - first) * QUAD, ROWS, COLS)


def window(refs, scales=None):
    def read(y):
        parts, left = [], 2 * PLANES
        for i, (ref, at) in enumerate(refs):
            n = min(left, ref.shape[0] - at)
            cells = ref[at : at + n, y, :]
            if scales is not None and scales[i] is not None:
                cells = cells * scales[i]
            parts.append(cells)
            left -= n
        while left > 0:
            n = min(left, parts[0].shape[0])
            parts.append(parts[0][:n])
            left -= n
        return jnp.concatenate(parts, axis=0)

    return read


def call(kernel, name, arrays, shared, ops, outs, scratch):
    out = [jax.ShapeDtypeStruct((n, ROWS, COLS), F32) for n in outs]
    return pl.pallas_call(
        kernel,
        out_shape=out,
        in_specs=[VMEM] * (len(arrays) + len(shared) + len(ops)),
        out_specs=[VMEM] * len(out),
        scratch_shapes=[pltpu.VMEM(shape, BF16) for shape in scratch],
        compiler_params=pltpu.CompilerParams(vmem_limit_bytes=20 * 2**20),
        cost_estimate=COST,
        name=name,
    )(*arrays, *shared, *ops)


def upper_ratio(step, own, above, shared, ops):
    parts = len(own) + len(above)
    tiles = PLANES // QUAD

    def kernel(*refs):
        slabs, ends, depth, row, col, ratio, spread, mixed = refs[parts:]
        live = ends[STEPS + step]
        scales = [None] * len(own) + [live] * len(above)
        cells = window([(ref, 0) for ref in refs[:parts]], scales)
        depth_pass(cells, depth, PLANES, spread)
        for t in range(tiles):
            row_pass(spread, row, mixed, t)
        value = slabs[step, PLANES:].astype(F32) / col_pass(mixed, col, 0, tiles)
        ratio[:HALF] = value[:HALF]
        ratio[HALF:] = value[HALF:] * live

    ranks = ops[0].shape[0]
    scratch = [(ranks, tiles, TILE, COLS), (tiles * TILE, ranks * COLS)]
    return call(kernel, "upper", own + above, shared, ops[0::2], [PLANES], scratch)[0]


def half_update(step, start, below, own, ratios, shared, ops):
    parts = len(below) + len(own)
    given = parts + len(ratios)

    def kernel(*refs):
        slabs, ends, depth_f, depth_a, row_f, row_a, col_f, col_a = refs[given : given + 8]
        ratio, updated, spread, mixed, spread_hi, mixed_hi, spread_lo, mixed_lo = refs[given + 8 :]
        live = ends[step]
        scales = [live] * len(below) + [None] * len(own)

        def divide(t):
            planes = slice(t * QUAD, (t + 1) * QUAD)
            seen = slabs[step, start + t * QUAD : start + (t + 1) * QUAD].astype(F32)
            value = seen / col_pass(mixed, col_f, t, t + 1)
            ratio[planes] = value * live if start == 0 else value

        def back(t, mixed_t):
            planes = slice(t * QUAD, (t + 1) * QUAD)
            updated[planes] = refs[parts - 1][planes] * col_pass(mixed_t, col_a, 0, 1)

        ratio_refs = [(ref, 0) for ref in refs[parts:given]]
        depth_pass(window([(ref, 0) for ref in refs[:parts]], scales), depth_f, HALF, spread)
        row_pass(spread, row_f, mixed, 1)
        divide(1)
        row_pass(spread, row_f, mixed, 0)
        depth_pass(window([(ratio, QUAD)] + ratio_refs), depth_a, QUAD, spread_hi)
        divide(0)
        row_pass(spread_hi, row_a, mixed_hi, 0)
        depth_pass(window([(ratio, 0)] + ratio_refs), depth_a, QUAD, spread_lo)
        back(1, mixed_hi)
        row_pass(spread_lo, row_a, mixed_lo, 0)
        back(0, mixed_lo)

    ranks = ops[0].shape[0]
    scratch = [
        shape
        for tiles in (2, 1, 1)
        for shape in ((ranks, tiles, TILE, COLS), (tiles * TILE, ranks * COLS))
    ]
    return call(kernel, "half", below + own + ratios, shared, ops, [HALF, HALF], scratch)


def placed_half(half, start, whole=None):
    extra = [] if whole is None else [whole]

    def kernel(*refs):
        half, out, sem = refs[0], refs[-2], refs[-1]
        copy = pltpu.make_async_copy(half, out.at[pl.ds(start, HALF)], sem)
        copy.start()
        copy.wait()

    return pl.pallas_call(
        kernel,
        out_shape=jax.ShapeDtypeStruct((PLANES, ROWS, COLS), F32),
        in_specs=[VMEM] + [HBM] * len(extra),
        out_specs=HBM,
        scratch_shapes=[pltpu.SemaphoreType.DMA],
        input_output_aliases={1: 0} if extra else {},
        compiler_params=pltpu.CompilerParams(vmem_limit_bytes=20 * 2**20),
        cost_estimate=COST,
        name="place",
    )(half, *extra)


def shards(
    images, start_estimate, view_order, psf_ranks, depth_taps, row_taps, col_taps, rank_weight
):
    count = lax.axis_size("view")

    def send(cells, by, relayed=None):
        pairs = []
        for i in range(count):
            way = relayed[1] if relayed and i % 4 == relayed[0] else by
            pairs.append((i, (i + way) % count))
        return lax.ppermute(cells, "view", pairs)

    above = [send(start_estimate, -1)]
    place = jnp.stack([lax.axis_index("view"), count]).astype(jnp.int32)
    ops, *shared = build(
        place, view_order, psf_ranks, rank_weight, depth_taps, row_taps, col_taps, images
    )
    own_lo, own_hi = start_estimate[:HALF], start_estimate[HALF:]
    early_hi, _ = lax.optimization_barrier((own_hi, ops[0]))
    below_hi = send(early_hi, 1)
    early_lo, _ = lax.optimization_barrier((own_lo, above[0]))
    below_lo = send(early_lo, 1)

    for step in range(STEPS):
        last = step == STEPS - 1
        ratio_up = upper_ratio(step, [own_lo, own_hi], above, shared, ops)
        ratio_mid, hi = half_update(
            step, HALF, [below_hi], [own_lo, own_hi], [ratio_up], shared, ops
        )
        next_hi = send(hi, 1 - STEPS, (1, 1)) if last else send(hi, 1)
        _, lo = half_update(
            step, 0, [below_lo, below_hi], [own_lo], [ratio_mid, ratio_up], shared, ops
        )
        above = [lo, hi]
        if last:
            next_hi, _ = lax.optimization_barrier((next_hi, lo))
            own_lo = send(lo, 1 - STEPS)
            own_hi = send(next_hi, 0, (2, -STEPS))
        else:
            own_lo, own_hi = send(lo, 1), next_hi
            below_hi = send(own_hi, 1)
            below_lo = send(own_lo, 1)
    return placed_half(own_hi, HALF, placed_half(own_lo, 0))


def solution(mesh):
    in_specs = (
        P(("groups", "view"), None, None, None, None),
        P(("groups", "view"), None, None),
        P(),
        P(),
        P(),
        P(),
        P(),
        P(),
    )
    out_specs = P(("groups", "view"), None, None)
    return jax.shard_map(shards, mesh=mesh, in_specs=in_specs, out_specs=out_specs, check_vma=False)
```

```python
import jax
import jax.numpy as jnp
from jax import lax
from jax.experimental import pallas as pl
from jax.experimental.pallas import tpu as pltpu
from jax.sharding import PartitionSpec as P

STEPS = 4
PLANES = 16
MARGIN = 8
HALF = 8
ROWS = 64
COLS = 256
GROUP = 8
QUAD = 4
TILE = 256

F32 = jnp.float32
BF16 = jnp.bfloat16
VMEM = pl.BlockSpec(memory_space=pltpu.VMEM)
SMEM = pl.BlockSpec(memory_space=pltpu.SMEM)
COST = pl.CostEstimate(flops=2**20, bytes_accessed=2**10, transcendentals=0)
HBM = pl.BlockSpec(memory_space=pltpu.HBM)


def dot(a, b):
    return jnp.dot(a, b, preferred_element_type=F32)


def iota(shape, dim):
    return lax.broadcasted_iota(jnp.int32, shape, dim)


def loop(count, body):
    def step(i, carry):
        body(i)
        return carry

    lax.fori_loop(0, count, step, 0)


def build_kernel(
    place, order, live, weight, depth_taps, row_taps, col_taps, images,
    depth_f, depth_a, row_f, row_a, col_f, col_a, *rest,
):
    slabs, ends = rest[:STEPS], rest[STEPS : 2 * STEPS]
    held, ahead, back, sems = rest[2 * STEPS :]
    copies = [
        pltpu.make_async_copy(images.at[0, step], slabs[step], sems.at[step])
        for step in range(STEPS)
    ]
    for copy in copies:
        copy.start()
    position, devices = place[0], place[1]
    for step in range(STEPS):
        block = lax.rem(position + (devices - step), devices)
        ends[step][0] = jnp.full((1, COLS), (block > 0).astype(F32))
        ends[step][1] = jnp.full((1, COLS), (block < devices - 1).astype(F32))
    views = order.shape[0]
    ranks, count = depth_taps.shape[1:]
    margin = count // 2
    view = order[lax.rem(position, views)]
    square = (TILE, TILE)

    def normal(taps):
        values = taps[view]
        return values / jnp.sum(values, axis=1, keepdims=True)

    rank = iota((ranks, 1), 0)
    weights = jnp.zeros((ranks, 1), F32)
    for r in range(ranks):
        weights = jnp.where(rank == r, weight[view, r], weights)
    weights = jnp.where(rank < live[view], weights, 0.0)
    weights = weights / jnp.sum(weights, axis=0, keepdims=True)

    def placed(values, place, to):
        held[...] = jnp.zeros(held.shape, F32)
        held[0:ranks, 0:count] = values
        k = iota((held.shape[1], TILE), 0)
        picks = (k < count) & (iota((held.shape[1], TILE), 1) == place(k))
        to[...] = dot(held[...].astype(BF16), picks.astype(F32).astype(BF16))

    def rolled(rows, r, n):
        full = jnp.broadcast_to(rows[pl.ds(r, 1)], (n, TILE))
        return pltpu.roll(full, 0, 1, stride=1, stride_axis=0)

    placed(normal(depth_taps) * weights, lambda k: GROUP * k, ahead)
    placed(normal(depth_taps) * weights, lambda k: GROUP * (count - 1 - k), back)

    def depth(r):
        depth_f[r] = rolled(ahead, r, PLANES * GROUP).astype(BF16)
        depth_a[r] = rolled(back, r, PLANES * GROUP).astype(BF16)

    loop(ranks, depth)
    i, j = iota(square, 0), iota(square, 1)
    near = jnp.abs(j - i) <= margin
    placed(normal(col_taps), lambda k: (margin - k) & (TILE - 1), ahead)
    placed(normal(col_taps), lambda k: (k - margin) & (TILE - 1), back)

    def col(r):
        col_f[r] = jnp.where(near, rolled(ahead, r, TILE), 0.0).astype(BF16)
        col_a[r] = jnp.where(near, rolled(back, r, TILE), 0.0).astype(BF16)

    loop(ranks, col)
    close = near & ((i >> 6) == (j >> 6))
    order_columns = ROWS * ((j >> 3) & (QUAD - 1)) + GROUP * (j >> 5) + (j & (GROUP - 1))
    order_columns = (i == order_columns).astype(F32).astype(BF16)
    placed(normal(row_taps), lambda k: (k - margin) & (TILE - 1), ahead)
    placed(normal(row_taps), lambda k: (margin - k) & (TILE - 1), back)

    def row(r):
        band = jnp.where(close, rolled(ahead, r, TILE), 0.0).astype(BF16)
        row_f[r] = dot(band, order_columns).astype(BF16)
        band = jnp.where(close, rolled(back, r, TILE), 0.0).astype(BF16)
        row_a[r] = dot(band, order_columns).astype(BF16)

    loop(ranks, row)
    for copy in copies:
        copy.wait()


def build(place, view_order, psf_ranks, rank_weight, depth_taps, row_taps, col_taps, images):
    ranks = depth_taps.shape[1]
    depth = jax.ShapeDtypeStruct((ranks, PLANES * GROUP, TILE), BF16)
    square = jax.ShapeDtypeStruct((ranks, TILE, TILE), BF16)
    slab = jax.ShapeDtypeStruct(images.shape[2:], BF16)
    ends = jax.ShapeDtypeStruct((2, 1, COLS), F32)
    out = pl.pallas_call(
        build_kernel,
        out_shape=[depth, depth] + [square] * 4 + [slab] * STEPS + [ends] * STEPS,
        in_specs=[SMEM] * 4 + [VMEM] * 3 + [HBM],
        out_specs=[VMEM] * (6 + 2 * STEPS),
        scratch_shapes=[
            pltpu.VMEM((8, 128), F32),
            pltpu.VMEM((8, TILE), F32),
            pltpu.VMEM((8, TILE), F32),
            pltpu.SemaphoreType.DMA((STEPS,)),
        ],
        compiler_params=pltpu.CompilerParams(vmem_limit_bytes=20 * 2**20),
        name="build",
    )(place, view_order, psf_ranks, rank_weight, depth_taps, row_taps, col_taps, images)
    return out[:6], out[6 : 6 + STEPS], out[6 + STEPS :]


def depth_pass(cells_of, op, planes, spread):
    ranks = op.shape[0]
    groups = ROWS // GROUP // 4
    lhs = op[:, 0 : planes * GROUP, :].reshape(ranks * planes * GROUP, TILE)

    def half(i):
        for g in range(groups):
            at = pl.multiple_of((i * groups + g) * GROUP, GROUP)
            cells = cells_of(pl.ds(at, GROUP))
            out = dot(lhs, cells.reshape(TILE, COLS).astype(BF16)).astype(BF16)
            out = out.reshape(ranks, planes // QUAD, QUAD * GROUP, COLS)
            to = pl.ds(pl.multiple_of(at * QUAD, QUAD * GROUP), QUAD * GROUP)
            spread[:, 0 : planes // QUAD, to, :] = out

    loop(4, half)


def row_pass(spread, op, mixed, t):
    rows = pl.ds(pl.multiple_of(t * TILE, TILE), TILE)
    for r in range(op.shape[0]):
        mixed[rows, r * COLS : (r + 1) * COLS] = dot(op[r], spread[r, t]).astype(BF16)


def col_pass(mixed, op, t):
    ranks = op.shape[0]
    rows = pl.ds(pl.multiple_of(t * TILE, TILE), TILE)
    return dot(mixed[rows, :], op[...].reshape(ranks * COLS, COLS)).reshape(QUAD, ROWS, COLS)


def window(refs, scales=None):
    def read(y):
        parts, left = [], 2 * PLANES
        for i, (ref, at) in enumerate(refs):
            n = min(left, ref.shape[0] - at)
            cells = ref[at : at + n, y, :]
            if scales is not None and scales[i] is not None:
                cells = cells * scales[i]
            parts.append(cells)
            left -= n
        while left > 0:
            n = min(left, parts[0].shape[0])
            parts.append(parts[0][:n])
            left -= n
        return jnp.concatenate(parts, axis=0)

    return read


def call(kernel, name, arrays, shared, ops, outs, scratch):
    out = [jax.ShapeDtypeStruct((n, ROWS, COLS), F32) for n in outs]
    return pl.pallas_call(
        kernel,
        out_shape=out,
        in_specs=[VMEM] * (len(arrays) + len(shared) + len(ops)),
        out_specs=[VMEM] * len(out),
        scratch_shapes=[pltpu.VMEM(shape, BF16) for shape in scratch],
        compiler_params=pltpu.CompilerParams(vmem_limit_bytes=20 * 2**20),
        cost_estimate=COST,
        name=name,
    )(*arrays, *shared, *ops)


def upper_ratio(own, above, shared, ops):
    parts = len(own) + len(above)
    tiles = PLANES // QUAD

    def kernel(*refs):
        slab, ends, depth, row, col, ratio, spread, mixed = refs[parts:]
        live = ends[1]
        scales = [None] * len(own) + [live] * len(above)
        cells = window([(ref, 0) for ref in refs[:parts]], scales)
        depth_pass(cells, depth, PLANES, spread)

        def pair(i):
            for t in (i,):
                row_pass(spread, row, mixed, t)
            for t in (i,):
                planes = pl.ds(t * QUAD, QUAD)
                seen = slab[pl.ds(PLANES + t * QUAD, QUAD)].astype(F32)
                ratio[planes] = seen / col_pass(mixed, col, t)

        loop(tiles, pair)
        ratio[HALF:] = ratio[HALF:] * live

    ranks = ops[0].shape[0]
    scratch = [(ranks, tiles, TILE, COLS), (tiles * TILE, ranks * COLS)]
    return call(kernel, "upper", own + above, shared, ops[0::2], [PLANES], scratch)[0]


def half_update(start, below, own, ratios, shared, ops):
    parts = len(below) + len(own)
    given = parts + len(ratios)
    tiles = HALF // QUAD

    def kernel(*refs):
        slab, ends, depth_f, depth_a, row_f, row_a, col_f, col_a = refs[given : given + 8]
        ratio, updated, spread, mixed = refs[given + 8 :]
        live = ends[0]
        scales = [live] * len(below) + [None] * len(own)

        def divide(t):
            row_pass(spread, row_f, mixed, t)
            seen = slab[pl.ds(start + t * QUAD, QUAD)].astype(F32)
            value = seen / col_pass(mixed, col_f, t)
            ratio[pl.ds(t * QUAD, QUAD)] = value * live if start == 0 else value

        def back(t):
            row_pass(spread, row_a, mixed, t)
            planes = pl.ds(t * QUAD, QUAD)
            updated[planes] = refs[parts - 1][planes] * col_pass(mixed, col_a, t)

        depth_pass(window([(ref, 0) for ref in refs[:parts]], scales), depth_f, HALF, spread)
        loop(tiles, divide)
        cells = window([(ref, 0) for ref in (ratio,) + refs[parts:given]])
        depth_pass(cells, depth_a, HALF, spread)
        loop(tiles, back)

    ranks = ops[0].shape[0]
    scratch = [(ranks, tiles, TILE, COLS), (tiles * TILE, ranks * COLS)]
    return call(kernel, "half", below + own + ratios, shared, ops, [HALF, HALF], scratch)


def placed_half(half, start, whole=None):
    extra = [] if whole is None else [whole]

    def kernel(*refs):
        half, out, sem = refs[0], refs[-2], refs[-1]
        copy = pltpu.make_async_copy(half, out.at[pl.ds(start, HALF)], sem)
        copy.start()
        copy.wait()

    return pl.pallas_call(
        kernel,
        out_shape=jax.ShapeDtypeStruct((PLANES, ROWS, COLS), F32),
        in_specs=[VMEM] + [HBM] * len(extra),
        out_specs=HBM,
        scratch_shapes=[pltpu.SemaphoreType.DMA],
        input_output_aliases={1: 0} if extra else {},
        compiler_params=pltpu.CompilerParams(vmem_limit_bytes=20 * 2**20),
        cost_estimate=COST,
        name="place",
    )(half, *extra)


def shards(
    images, start_estimate, view_order, psf_ranks, depth_taps, row_taps, col_taps, rank_weight
):
    count = lax.axis_size("view")

    def send(cells, by, relayed=None, skip=()):
        pairs = []
        for i in range(count):
            way = relayed[1] if relayed and i % 4 == relayed[0] else by
            if i not in skip:
                pairs.append((i, (i + way) % count))
        return lax.ppermute(cells, "view", pairs)

    above = [send(start_estimate, -1)]
    place = jnp.stack([lax.axis_index("view"), count]).astype(jnp.int32)
    ops, slabs, ends = build(
        place, view_order, psf_ranks, rank_weight, depth_taps, row_taps, col_taps, images
    )
    own_lo, own_hi = start_estimate[:HALF], start_estimate[HALF:]
    early_hi, _ = lax.optimization_barrier((own_hi, ops[0]))
    below_hi = send(early_hi, 1, skip=(count - 1,))
    early_lo, _ = lax.optimization_barrier((own_lo, above[0]))
    below_lo = send(early_lo, 1)

    for step in range(STEPS):
        last = step == STEPS - 1
        shared = [slabs[step], ends[step]]
        ratio_up = upper_ratio([own_lo, own_hi], above, shared, ops)
        ratio_mid, hi = half_update(HALF, [below_hi], [own_lo, own_hi], [ratio_up], shared, ops)
        next_hi = send(hi, 1 - STEPS, (1, 1)) if last else send(hi, 1)
        _, lo = half_update(
            0, [below_lo, below_hi], [own_lo], [ratio_mid, ratio_up], shared, ops
        )
        above = [lo, hi]
        if last:
            next_hi, _ = lax.optimization_barrier((next_hi, lo))
            own_lo = send(lo, 1 - STEPS)
            own_hi = send(next_hi, 0, (2, -STEPS))
        else:
            own_lo, own_hi = send(lo, 1), next_hi
            below_hi = send(own_hi, 1)
            below_lo = send(own_lo, 1)
    return placed_half(own_hi, HALF, placed_half(own_lo, 0))


def solution(mesh):
    in_specs = (
        P(("groups", "view"), None, None, None, None),
        P(("groups", "view"), None, None),
        P(),
        P(),
        P(),
        P(),
        P(),
        P(),
    )
    out_specs = P(("groups", "view"), None, None)
    return jax.shard_map(shards, mesh=mesh, in_specs=in_specs, out_specs=out_specs, check_vma=False)
```

```python
import jax
import jax.numpy as jnp
from jax import lax
from jax.experimental import pallas as pl
from jax.experimental.pallas import tpu as pltpu
from jax.sharding import PartitionSpec as P

STEPS = 4
PLANES = 16
MARGIN = 8
HALF = 8
ROWS = 64
COLS = 256
GROUP = 8
QUAD = 4
TILE = 256

F32 = jnp.float32
BF16 = jnp.bfloat16
VMEM = pl.BlockSpec(memory_space=pltpu.VMEM)
SMEM = pl.BlockSpec(memory_space=pltpu.SMEM)
COST = pl.CostEstimate(flops=2**20, bytes_accessed=2**10, transcendentals=0)
HBM = pl.BlockSpec(memory_space=pltpu.HBM)


def dot(a, b):
    return jnp.dot(a, b, preferred_element_type=F32)


def iota(shape, dim):
    return lax.broadcasted_iota(jnp.int32, shape, dim)


def loop(count, body):
    def step(i, carry):
        body(i)
        return carry

    lax.fori_loop(0, count, step, 0)


def build_kernel(
    place, order, live, weight, depth_taps, row_taps, col_taps, images,
    depth_f, depth_a, row_f, row_a, col_f, col_a, *rest,
):
    slabs, ends = rest[:STEPS], rest[STEPS : 2 * STEPS]
    held, ahead, back, sems = rest[2 * STEPS :]
    copies = [
        pltpu.make_async_copy(images.at[0, step], slabs[step], sems.at[step])
        for step in range(STEPS)
    ]
    for copy in copies:
        copy.start()
    position, devices = place[0], place[1]
    for step in range(STEPS):
        block = lax.rem(position + (devices - step), devices)
        ends[step][0] = jnp.full((1, COLS), (block > 0).astype(F32))
        ends[step][1] = jnp.full((1, COLS), (block < devices - 1).astype(F32))
    views = order.shape[0]
    ranks, count = depth_taps.shape[1:]
    margin = count // 2
    view = order[lax.rem(position, views)]
    square = (TILE, TILE)

    def normal(taps):
        values = taps[view]
        return values / jnp.sum(values, axis=1, keepdims=True)

    rank = iota((ranks, 1), 0)
    weights = jnp.zeros((ranks, 1), F32)
    for r in range(ranks):
        weights = jnp.where(rank == r, weight[view, r], weights)
    weights = jnp.where(rank < live[view], weights, 0.0)
    weights = weights / jnp.sum(weights, axis=0, keepdims=True)

    def placed(values, place, to):
        held[...] = jnp.zeros(held.shape, F32)
        held[0:ranks, 0:count] = values
        k = iota((held.shape[1], TILE), 0)
        picks = (k < count) & (iota((held.shape[1], TILE), 1) == place(k))
        to[...] = dot(held[...].astype(BF16), picks.astype(F32).astype(BF16))

    def rolled(rows, r, n):
        full = jnp.broadcast_to(rows[pl.ds(r, 1)], (n, TILE))
        return pltpu.roll(full, 0, 1, stride=1, stride_axis=0)

    placed(normal(depth_taps) * weights, lambda k: GROUP * k, ahead)
    placed(normal(depth_taps) * weights, lambda k: GROUP * (count - 1 - k), back)

    def depth(r):
        depth_f[r] = rolled(ahead, r, PLANES * GROUP).astype(BF16)
        depth_a[r] = rolled(back, r, PLANES * GROUP).astype(BF16)

    loop(ranks, depth)
    i, j = iota(square, 0), iota(square, 1)
    near = jnp.abs(j - i) <= margin
    placed(normal(col_taps), lambda k: (margin - k) & (TILE - 1), ahead)
    placed(normal(col_taps), lambda k: (k - margin) & (TILE - 1), back)

    def col(r):
        col_f[r] = jnp.where(near, rolled(ahead, r, TILE), 0.0).astype(BF16)
        col_a[r] = jnp.where(near, rolled(back, r, TILE), 0.0).astype(BF16)

    loop(ranks, col)
    close = near & ((i >> 6) == (j >> 6))
    order_columns = ROWS * ((j >> 3) & (QUAD - 1)) + GROUP * (j >> 5) + (j & (GROUP - 1))
    order_columns = (i == order_columns).astype(F32).astype(BF16)
    placed(normal(row_taps), lambda k: (k - margin) & (TILE - 1), ahead)
    placed(normal(row_taps), lambda k: (margin - k) & (TILE - 1), back)

    def row(r):
        band = jnp.where(close, rolled(ahead, r, TILE), 0.0).astype(BF16)
        row_f[r] = dot(band, order_columns).astype(BF16)
        band = jnp.where(close, rolled(back, r, TILE), 0.0).astype(BF16)
        row_a[r] = dot(band, order_columns).astype(BF16)

    loop(ranks, row)
    for copy in copies:
        copy.wait()


def build(place, view_order, psf_ranks, rank_weight, depth_taps, row_taps, col_taps, images):
    ranks = depth_taps.shape[1]
    depth = jax.ShapeDtypeStruct((ranks, PLANES * GROUP, TILE), BF16)
    square = jax.ShapeDtypeStruct((ranks, TILE, TILE), BF16)
    slab = jax.ShapeDtypeStruct(images.shape[2:], BF16)
    ends = jax.ShapeDtypeStruct((2, 1, COLS), F32)
    out = pl.pallas_call(
        build_kernel,
        out_shape=[depth, depth] + [square] * 4 + [slab] * STEPS + [ends] * STEPS,
        in_specs=[SMEM] * 4 + [VMEM] * 3 + [HBM],
        out_specs=[VMEM] * (6 + 2 * STEPS),
        scratch_shapes=[
            pltpu.VMEM((8, 128), F32),
            pltpu.VMEM((8, TILE), F32),
            pltpu.VMEM((8, TILE), F32),
            pltpu.SemaphoreType.DMA((STEPS,)),
        ],
        compiler_params=pltpu.CompilerParams(vmem_limit_bytes=20 * 2**20),
        name="build",
    )(place, view_order, psf_ranks, rank_weight, depth_taps, row_taps, col_taps, images)
    return out[:6], out[6 : 6 + STEPS], out[6 + STEPS :]


def depth_pass(cells_of, op, planes, spread):
    ranks = op.shape[0]
    groups = ROWS // GROUP // 4
    lhs = op[:, 0 : planes * GROUP, :].reshape(ranks * planes * GROUP, TILE)

    def half(i):
        for g in range(groups):
            at = pl.multiple_of((i * groups + g) * GROUP, GROUP)
            cells = cells_of(pl.ds(at, GROUP))
            out = dot(lhs, cells.reshape(TILE, COLS).astype(BF16)).astype(BF16)
            out = out.reshape(ranks, planes // QUAD, QUAD * GROUP, COLS)
            to = pl.ds(pl.multiple_of(at * QUAD, QUAD * GROUP), QUAD * GROUP)
            spread[:, 0 : planes // QUAD, to, :] = out

    loop(4, half)


def row_pass(spread, op, mixed, t):
    rows = pl.ds(pl.multiple_of(t * TILE, TILE), TILE)
    for r in range(op.shape[0]):
        mixed[rows, r * COLS : (r + 1) * COLS] = dot(op[r], spread[r, t]).astype(BF16)


def col_pass(mixed, op, t):
    ranks = op.shape[0]
    rows = pl.ds(pl.multiple_of(t * TILE, TILE), TILE)
    return dot(mixed[rows, :], op[...].reshape(ranks * COLS, COLS)).reshape(QUAD, ROWS, COLS)


def depth_whole(cells_of, op, planes, spread):
    ranks = op.shape[0]
    lhs = op[:, 0 : planes * GROUP, :].reshape(ranks * planes * GROUP, TILE)
    for g in range(ROWS // GROUP):
        cells = cells_of(slice(g * GROUP, (g + 1) * GROUP))
        out = dot(lhs, cells.reshape(TILE, COLS).astype(BF16)).astype(BF16)
        out = out.reshape(ranks, planes // QUAD, QUAD * GROUP, COLS)
        spread[:, :, g * QUAD * GROUP : (g + 1) * QUAD * GROUP, :] = out


def row_whole(spread, op, mixed, t):
    for r in range(op.shape[0]):
        mixed[t * TILE : (t + 1) * TILE, r * COLS : (r + 1) * COLS] = dot(
            op[r], spread[r, t]
        ).astype(BF16)


def col_whole(mixed, op, t):
    ranks = op.shape[0]
    out = dot(mixed[t * TILE : (t + 1) * TILE, :], op[...].reshape(ranks * COLS, COLS))
    return out.reshape(QUAD, ROWS, COLS)


def window(refs, scales=None):
    def read(y):
        parts, left = [], 2 * PLANES
        for i, (ref, at) in enumerate(refs):
            n = min(left, ref.shape[0] - at)
            cells = ref[at : at + n, y, :]
            if scales is not None and scales[i] is not None:
                cells = cells * scales[i]
            parts.append(cells)
            left -= n
        while left > 0:
            n = min(left, parts[0].shape[0])
            parts.append(parts[0][:n])
            left -= n
        return jnp.concatenate(parts, axis=0)

    return read


def call(kernel, name, arrays, shared, ops, outs, scratch):
    out = [jax.ShapeDtypeStruct((n, ROWS, COLS), F32) for n in outs]
    return pl.pallas_call(
        kernel,
        out_shape=out,
        in_specs=[VMEM] * (len(arrays) + len(shared) + len(ops)),
        out_specs=[VMEM] * len(out),
        scratch_shapes=[pltpu.VMEM(shape, BF16) for shape in scratch],
        compiler_params=pltpu.CompilerParams(vmem_limit_bytes=20 * 2**20),
        cost_estimate=COST,
        name=name,
    )(*arrays, *shared, *ops)


def upper_ratio(own, above, shared, ops):
    parts = len(own) + len(above)
    tiles = PLANES // QUAD

    def kernel(*refs):
        slab, ends, depth, row, col, ratio, spread, mixed = refs[parts:]
        live = ends[1]
        scales = [None] * len(own) + [live] * len(above)
        cells = window([(ref, 0) for ref in refs[:parts]], scales)
        depth_pass(cells, depth, PLANES, spread)

        def pair(i):
            for t in (i,):
                row_pass(spread, row, mixed, t)
            for t in (i,):
                planes = pl.ds(t * QUAD, QUAD)
                seen = slab[pl.ds(PLANES + t * QUAD, QUAD)].astype(F32)
                ratio[planes] = seen / col_pass(mixed, col, t)

        loop(tiles, pair)
        ratio[HALF:] = ratio[HALF:] * live

    ranks = ops[0].shape[0]
    scratch = [(ranks, tiles, TILE, COLS), (tiles * TILE, ranks * COLS)]
    return call(kernel, "upper", own + above, shared, ops[0::2], [PLANES], scratch)[0]


def half_update(start, below, own, ratios, shared, ops):
    parts = len(below) + len(own)
    given = parts + len(ratios)

    def kernel(*refs):
        slab, ends, depth_f, depth_a, row_f, row_a, col_f, col_a = refs[given : given + 8]
        ratio, updated, spread, mixed, spread_hi, mixed_hi, spread_lo, mixed_lo = refs[given + 8 :]
        live = ends[0]
        scales = [live] * len(below) + [None] * len(own)

        def divide(t):
            planes = slice(t * QUAD, (t + 1) * QUAD)
            seen = slab[start + t * QUAD : start + (t + 1) * QUAD].astype(F32)
            value = seen / col_whole(mixed, col_f, t)
            ratio[planes] = value * live if start == 0 else value

        def back(t, mixed_t):
            planes = slice(t * QUAD, (t + 1) * QUAD)
            updated[planes] = refs[parts - 1][planes] * col_whole(mixed_t, col_a, 0)

        ratio_refs = [(ref, 0) for ref in refs[parts:given]]
        depth_whole(window([(ref, 0) for ref in refs[:parts]], scales), depth_f, HALF, spread)
        row_whole(spread, row_f, mixed, 1)
        divide(1)
        row_whole(spread, row_f, mixed, 0)
        depth_whole(window([(ratio, QUAD)] + ratio_refs), depth_a, QUAD, spread_hi)
        divide(0)
        row_whole(spread_hi, row_a, mixed_hi, 0)
        depth_whole(window([(ratio, 0)] + ratio_refs), depth_a, QUAD, spread_lo)
        back(1, mixed_hi)
        row_whole(spread_lo, row_a, mixed_lo, 0)
        back(0, mixed_lo)

    ranks = ops[0].shape[0]
    scratch = [
        shape
        for tiles in (2, 1, 1)
        for shape in ((ranks, tiles, TILE, COLS), (tiles * TILE, ranks * COLS))
    ]
    return call(kernel, "half", below + own + ratios, shared, ops, [HALF, HALF], scratch)


def placed_half(half, start, whole=None):
    extra = [] if whole is None else [whole]

    def kernel(*refs):
        half, out, sem = refs[0], refs[-2], refs[-1]
        copy = pltpu.make_async_copy(half, out.at[pl.ds(start, HALF)], sem)
        copy.start()
        copy.wait()

    return pl.pallas_call(
        kernel,
        out_shape=jax.ShapeDtypeStruct((PLANES, ROWS, COLS), F32),
        in_specs=[VMEM] + [HBM] * len(extra),
        out_specs=HBM,
        scratch_shapes=[pltpu.SemaphoreType.DMA],
        input_output_aliases={1: 0} if extra else {},
        compiler_params=pltpu.CompilerParams(vmem_limit_bytes=20 * 2**20),
        cost_estimate=COST,
        name="place",
    )(half, *extra)


def shards(
    images, start_estimate, view_order, psf_ranks, depth_taps, row_taps, col_taps, rank_weight
):
    count = lax.axis_size("view")

    def send(cells, by, relayed=None, skip=()):
        pairs = []
        for i in range(count):
            way = relayed[1] if relayed and i % 4 == relayed[0] else by
            if i not in skip:
                pairs.append((i, (i + way) % count))
        return lax.ppermute(cells, "view", pairs)

    above = [send(start_estimate, -1)]
    place = jnp.stack([lax.axis_index("view"), count]).astype(jnp.int32)
    ops, slabs, ends = build(
        place, view_order, psf_ranks, rank_weight, depth_taps, row_taps, col_taps, images
    )
    own_lo, own_hi = start_estimate[:HALF], start_estimate[HALF:]
    early_hi, _ = lax.optimization_barrier((own_hi, ops[0]))
    below_hi = send(early_hi, 1, skip=(count - 1,))
    early_lo, _ = lax.optimization_barrier((own_lo, above[0]))
    below_lo = send(early_lo, 1)

    for step in range(STEPS):
        last = step == STEPS - 1
        shared = [slabs[step], ends[step]]
        ratio_up = upper_ratio([own_lo, own_hi], above, shared, ops)
        ratio_mid, hi = half_update(HALF, [below_hi], [own_lo, own_hi], [ratio_up], shared, ops)
        next_hi = send(hi, 1 - STEPS, (1, 1)) if last else send(hi, 1)
        _, lo = half_update(
            0, [below_lo, below_hi], [own_lo], [ratio_mid, ratio_up], shared, ops
        )
        above = [lo, hi]
        if last:
            next_hi, _ = lax.optimization_barrier((next_hi, lo))
            own_lo = send(lo, 1 - STEPS)
            own_hi = send(next_hi, 0, (2, -STEPS))
        else:
            own_lo, own_hi = send(lo, 1), next_hi
            below_hi = send(own_hi, 1)
            below_lo = send(own_lo, 1)
    return placed_half(own_hi, HALF, placed_half(own_lo, 0))


def solution(mesh):
    in_specs = (
        P(("groups", "view"), None, None, None, None),
        P(("groups", "view"), None, None),
        P(),
        P(),
        P(),
        P(),
        P(),
        P(),
    )
    out_specs = P(("groups", "view"), None, None)
    return jax.shard_map(shards, mesh=mesh, in_specs=in_specs, out_specs=out_specs, check_vma=False)
```

```python
import jax
import jax.numpy as jnp
from jax import lax
from jax.experimental import pallas as pl
from jax.experimental.pallas import tpu as pltpu
from jax.sharding import PartitionSpec as P

STEPS = 4
PLANES = 16
MARGIN = 8
HALF = 8
ROWS = 64
COLS = 256
GROUP = 8
QUAD = 4
TILE = 256

F32 = jnp.float32
BF16 = jnp.bfloat16
VMEM = pl.BlockSpec(memory_space=pltpu.VMEM)
SMEM = pl.BlockSpec(memory_space=pltpu.SMEM)
COST = pl.CostEstimate(flops=2**20, bytes_accessed=2**10, transcendentals=0)
HBM = pl.BlockSpec(memory_space=pltpu.HBM)


def dot(a, b):
    return jnp.dot(a, b, preferred_element_type=F32)


def iota(shape, dim):
    return lax.broadcasted_iota(jnp.int32, shape, dim)


def loop(count, body):
    def step(i, carry):
        body(i)
        return carry

    lax.fori_loop(0, count, step, 0)


def build_kernel(
    place, order, live, weight, depth_taps, row_taps, col_taps, images,
    depth_f, depth_a, row_f, row_a, col_f, col_a, *rest,
):
    slabs, ends = rest[:STEPS], rest[STEPS : 2 * STEPS]
    held, ahead, back, sems = rest[2 * STEPS :]
    copies = [
        pltpu.make_async_copy(images.at[0, step], slabs[step], sems.at[step])
        for step in range(STEPS)
    ]
    for copy in copies:
        copy.start()
    position, devices = place[0], place[1]
    for step in range(STEPS):
        block = lax.rem(position + (devices - step), devices)
        ends[step][0] = jnp.full((1, COLS), (block > 0).astype(F32))
        ends[step][1] = jnp.full((1, COLS), (block < devices - 1).astype(F32))
    views = order.shape[0]
    ranks, count = depth_taps.shape[1:]
    margin = count // 2
    view = order[lax.rem(position, views)]
    square = (TILE, TILE)

    def normal(taps):
        values = taps[view]
        return values / jnp.sum(values, axis=1, keepdims=True)

    rank = iota((ranks, 1), 0)
    weights = jnp.zeros((ranks, 1), F32)
    for r in range(ranks):
        weights = jnp.where(rank == r, weight[view, r], weights)
    weights = jnp.where(rank < live[view], weights, 0.0)
    weights = weights / jnp.sum(weights, axis=0, keepdims=True)

    def placed(values, place, to):
        held[...] = jnp.zeros(held.shape, F32)
        held[0:ranks, 0:count] = values
        k = iota((held.shape[1], TILE), 0)
        picks = (k < count) & (iota((held.shape[1], TILE), 1) == place(k))
        to[...] = dot(held[...].astype(BF16), picks.astype(F32).astype(BF16))

    def rolled(rows, r, n):
        full = jnp.broadcast_to(rows[pl.ds(r, 1)], (n, TILE))
        return pltpu.roll(full, 0, 1, stride=1, stride_axis=0)

    placed(normal(depth_taps) * weights, lambda k: GROUP * k, ahead)
    placed(normal(depth_taps) * weights, lambda k: GROUP * (count - 1 - k), back)

    def depth(r):
        depth_f[r] = rolled(ahead, r, PLANES * GROUP).astype(BF16)
        depth_a[r] = rolled(back, r, PLANES * GROUP).astype(BF16)

    loop(ranks, depth)
    i, j = iota(square, 0), iota(square, 1)
    near = jnp.abs(j - i) <= margin
    placed(normal(col_taps), lambda k: (margin - k) & (TILE - 1), ahead)
    placed(normal(col_taps), lambda k: (k - margin) & (TILE - 1), back)

    def col(r):
        col_f[r] = jnp.where(near, rolled(ahead, r, TILE), 0.0).astype(BF16)
        col_a[r] = jnp.where(near, rolled(back, r, TILE), 0.0).astype(BF16)

    loop(ranks, col)
    close = near & ((i >> 6) == (j >> 6))
    order_columns = ROWS * ((j >> 3) & (QUAD - 1)) + GROUP * (j >> 5) + (j & (GROUP - 1))
    order_columns = (i == order_columns).astype(F32).astype(BF16)
    placed(normal(row_taps), lambda k: (k - margin) & (TILE - 1), ahead)
    placed(normal(row_taps), lambda k: (margin - k) & (TILE - 1), back)

    def row(r):
        band = jnp.where(close, rolled(ahead, r, TILE), 0.0).astype(BF16)
        row_f[r] = dot(band, order_columns).astype(BF16)
        band = jnp.where(close, rolled(back, r, TILE), 0.0).astype(BF16)
        row_a[r] = dot(band, order_columns).astype(BF16)

    loop(ranks, row)
    for copy in copies:
        copy.wait()


def build(place, view_order, psf_ranks, rank_weight, depth_taps, row_taps, col_taps, images):
    ranks = depth_taps.shape[1]
    depth = jax.ShapeDtypeStruct((ranks, PLANES * GROUP, TILE), BF16)
    square = jax.ShapeDtypeStruct((ranks, TILE, TILE), BF16)
    slab = jax.ShapeDtypeStruct(images.shape[2:], BF16)
    ends = jax.ShapeDtypeStruct((2, 1, COLS), F32)
    out = pl.pallas_call(
        build_kernel,
        out_shape=[depth, depth] + [square] * 4 + [slab] * STEPS + [ends] * STEPS,
        in_specs=[SMEM] * 4 + [VMEM] * 3 + [HBM],
        out_specs=[VMEM] * (6 + 2 * STEPS),
        scratch_shapes=[
            pltpu.VMEM((8, 128), F32),
            pltpu.VMEM((8, TILE), F32),
            pltpu.VMEM((8, TILE), F32),
            pltpu.SemaphoreType.DMA((STEPS,)),
        ],
        compiler_params=pltpu.CompilerParams(vmem_limit_bytes=20 * 2**20),
        name="build",
    )(place, view_order, psf_ranks, rank_weight, depth_taps, row_taps, col_taps, images)
    return out[:6], out[6 : 6 + STEPS], out[6 + STEPS :]


def depth_pass(cells_of, op, planes, spread):
    ranks = op.shape[0]
    groups = ROWS // GROUP // 4
    lhs = op[:, 0 : planes * GROUP, :].reshape(ranks * planes * GROUP, TILE)

    def half(i):
        for g in range(groups):
            at = pl.multiple_of((i * groups + g) * GROUP, GROUP)
            cells = cells_of(pl.ds(at, GROUP))
            out = dot(lhs, cells.reshape(TILE, COLS).astype(BF16)).astype(BF16)
            out = out.reshape(ranks, planes // QUAD, QUAD * GROUP, COLS)
            to = pl.ds(pl.multiple_of(at * QUAD, QUAD * GROUP), QUAD * GROUP)
            spread[:, 0 : planes // QUAD, to, :] = out

    loop(4, half)


def row_pass(spread, op, mixed, t):
    rows = pl.ds(pl.multiple_of(t * TILE, TILE), TILE)
    for r in range(op.shape[0]):
        mixed[rows, r * COLS : (r + 1) * COLS] = dot(op[r], spread[r, t]).astype(BF16)


def col_pass(mixed, op, t):
    ranks = op.shape[0]
    rows = pl.ds(pl.multiple_of(t * TILE, TILE), TILE)
    return dot(mixed[rows, :], op[...].reshape(ranks * COLS, COLS)).reshape(QUAD, ROWS, COLS)


def depth_whole(cells_of, op, planes, spread):
    ranks = op.shape[0]
    lhs = op[:, 0 : planes * GROUP, :].reshape(ranks * planes * GROUP, TILE)
    for g in range(ROWS // GROUP):
        cells = cells_of(slice(g * GROUP, (g + 1) * GROUP))
        out = dot(lhs, cells.reshape(TILE, COLS).astype(BF16)).astype(BF16)
        out = out.reshape(ranks, planes // QUAD, QUAD * GROUP, COLS)
        spread[:, :, g * QUAD * GROUP : (g + 1) * QUAD * GROUP, :] = out


def row_whole(spread, op, mixed, t):
    for r in range(op.shape[0]):
        mixed[t * TILE : (t + 1) * TILE, r * COLS : (r + 1) * COLS] = dot(
            op[r], spread[r, t]
        ).astype(BF16)


def col_whole(mixed, op, t):
    ranks = op.shape[0]
    out = dot(mixed[t * TILE : (t + 1) * TILE, :], op[...].reshape(ranks * COLS, COLS))
    return out.reshape(QUAD, ROWS, COLS)


def window(refs, scales=None):
    def read(y):
        parts, left = [], 2 * PLANES
        for i, (ref, at) in enumerate(refs):
            n = min(left, ref.shape[0] - at)
            cells = ref[at : at + n, y, :]
            if scales is not None and scales[i] is not None:
                cells = cells * scales[i]
            parts.append(cells)
            left -= n
        while left > 0:
            n = min(left, parts[0].shape[0])
            parts.append(parts[0][:n])
            left -= n
        return jnp.concatenate(parts, axis=0)

    return read


def call(kernel, name, arrays, shared, ops, outs, scratch):
    out = [jax.ShapeDtypeStruct((n, ROWS, COLS), F32) for n in outs]
    return pl.pallas_call(
        kernel,
        out_shape=out,
        in_specs=[VMEM] * (len(arrays) + len(shared) + len(ops)),
        out_specs=[VMEM] * len(out),
        scratch_shapes=[pltpu.VMEM(shape, BF16) for shape in scratch],
        compiler_params=pltpu.CompilerParams(vmem_limit_bytes=20 * 2**20),
        cost_estimate=COST,
        name=name,
    )(*arrays, *shared, *ops)


def upper_ratio(own, above, shared, ops):
    parts = len(own) + len(above)
    tiles = PLANES // QUAD

    def kernel(*refs):
        slab, ends, depth, row, col, ratio, spread, mixed = refs[parts:]
        live = ends[1]
        scales = [None] * len(own) + [live] * len(above)
        cells = window([(ref, 0) for ref in refs[:parts]], scales)
        depth_pass(cells, depth, PLANES, spread)

        def pair(i):
            for t in (i,):
                row_pass(spread, row, mixed, t)
            for t in (i,):
                planes = pl.ds(t * QUAD, QUAD)
                seen = slab[pl.ds(PLANES + t * QUAD, QUAD)].astype(F32)
                ratio[planes] = seen / col_pass(mixed, col, t)

        loop(tiles, pair)
        ratio[HALF:] = ratio[HALF:] * live

    ranks = ops[0].shape[0]
    scratch = [(ranks, tiles, TILE, COLS), (tiles * TILE, ranks * COLS)]
    return call(kernel, "upper", own + above, shared, ops[0::2], [PLANES], scratch)[0]


def half_update(start, below, own, ratios, shared, ops):
    parts = len(below) + len(own)
    given = parts + len(ratios)

    def kernel(*refs):
        slab, ends, depth_f, depth_a, row_f, row_a, col_f, col_a = refs[given : given + 8]
        ratio, updated, spread, mixed, spread_hi, mixed_hi, spread_lo, mixed_lo = refs[given + 8 :]
        live = ends[0]
        scales = [live] * len(below) + [None] * len(own)

        def divide(t):
            planes = slice(t * QUAD, (t + 1) * QUAD)
            seen = slab[start + t * QUAD : start + (t + 1) * QUAD].astype(F32)
            value = seen / col_whole(mixed, col_f, t)
            ratio[planes] = value * live if start == 0 else value

        def back(t, mixed_t):
            planes = slice(t * QUAD, (t + 1) * QUAD)
            updated[planes] = refs[parts - 1][planes] * col_whole(mixed_t, col_a, 0)

        ratio_refs = [(ref, 0) for ref in refs[parts:given]]
        depth_whole(window([(ref, 0) for ref in refs[:parts]], scales), depth_f, HALF, spread)
        row_whole(spread, row_f, mixed, 1)
        divide(1)
        row_whole(spread, row_f, mixed, 0)
        depth_whole(window([(ratio, QUAD)] + ratio_refs), depth_a, QUAD, spread_hi)
        divide(0)
        row_whole(spread_hi, row_a, mixed_hi, 0)
        depth_whole(window([(ratio, 0)] + ratio_refs), depth_a, QUAD, spread_lo)
        back(1, mixed_hi)
        row_whole(spread_lo, row_a, mixed_lo, 0)
        back(0, mixed_lo)

    ranks = ops[0].shape[0]
    scratch = [
        shape
        for tiles in (2, 1, 1)
        for shape in ((ranks, tiles, TILE, COLS), (tiles * TILE, ranks * COLS))
    ]
    return call(kernel, "half", below + own + ratios, shared, ops, [HALF, HALF], scratch)


def whole(lo, hi):
    def kernel(lo, hi, out, sems):
        copies = [
            pltpu.make_async_copy(half, out.at[pl.ds(i * HALF, HALF)], sems.at[i])
            for i, half in enumerate((lo, hi))
        ]
        for copy in copies:
            copy.start()
        for copy in copies:
            copy.wait()

    return pl.pallas_call(
        kernel,
        out_shape=jax.ShapeDtypeStruct((PLANES, ROWS, COLS), F32),
        in_specs=[VMEM] * 2,
        out_specs=HBM,
        scratch_shapes=[pltpu.SemaphoreType.DMA((2,))],
        compiler_params=pltpu.CompilerParams(vmem_limit_bytes=20 * 2**20),
        cost_estimate=COST,
        name="whole",
    )(lo, hi)


def shards(
    images, start_estimate, view_order, psf_ranks, depth_taps, row_taps, col_taps, rank_weight
):
    count = lax.axis_size("view")

    def send(cells, by, relayed=None, skip=()):
        pairs = []
        for i in range(count):
            way = relayed[1] if relayed and i % 4 == relayed[0] else by
            if i not in skip:
                pairs.append((i, (i + way) % count))
        return lax.ppermute(cells, "view", pairs)

    above = [send(start_estimate, -1)]
    place = jnp.stack([lax.axis_index("view"), count]).astype(jnp.int32)
    ops, slabs, ends = build(
        place, view_order, psf_ranks, rank_weight, depth_taps, row_taps, col_taps, images
    )
    own_lo, own_hi = start_estimate[:HALF], start_estimate[HALF:]
    early_hi, _ = lax.optimization_barrier((own_hi, ops[0]))
    below_hi = send(early_hi, 1, skip=(count - 1,))
    early_lo, _ = lax.optimization_barrier((own_lo, above[0]))
    below_lo = send(early_lo, 1, skip=(count - 1,))

    for step in range(STEPS):
        last = step == STEPS - 1
        shared = [slabs[step], ends[step]]
        ratio_up = upper_ratio([own_lo, own_hi], above, shared, ops)
        ratio_mid, hi = half_update(HALF, [below_hi], [own_lo, own_hi], [ratio_up], shared, ops)
        next_hi = send(hi, 1 - STEPS, (1, 1)) if last else send(hi, 1)
        _, lo = half_update(
            0, [below_lo, below_hi], [own_lo], [ratio_mid, ratio_up], shared, ops
        )
        above = [lo, hi]
        if last:
            next_hi, _ = lax.optimization_barrier((next_hi, lo))
            own_lo = send(lo, 1 - STEPS)
            own_hi = send(next_hi, 0, (2, -STEPS))
        else:
            own_lo, own_hi = send(lo, 1), next_hi
            below_hi = send(own_hi, 1)
            below_lo = send(own_lo, 1)
    return whole(own_lo, own_hi)


def solution(mesh):
    in_specs = (
        P(("groups", "view"), None, None, None, None),
        P(("groups", "view"), None, None),
        P(),
        P(),
        P(),
        P(),
        P(),
        P(),
    )
    out_specs = P(("groups", "view"), None, None)
    return jax.shard_map(shards, mesh=mesh, in_specs=in_specs, out_specs=out_specs, check_vma=False)
```

```python
import jax
import jax.numpy as jnp
from jax import lax
from jax.experimental import pallas as pl
from jax.experimental.pallas import tpu as pltpu
from jax.sharding import PartitionSpec as P

STEPS = 4
PLANES = 16
MARGIN = 8
HALF = 8
ROWS = 64
COLS = 256
GROUP = 8
QUAD = 4
TILE = 256

F32 = jnp.float32
BF16 = jnp.bfloat16
VMEM = pl.BlockSpec(memory_space=pltpu.VMEM)
SMEM = pl.BlockSpec(memory_space=pltpu.SMEM)
COST = pl.CostEstimate(flops=2**20, bytes_accessed=2**10, transcendentals=0)
HBM = pl.BlockSpec(memory_space=pltpu.HBM)


def dot(a, b):
    return jnp.dot(a, b, preferred_element_type=F32)


def iota(shape, dim):
    return lax.broadcasted_iota(jnp.int32, shape, dim)


def loop(count, body):
    def step(i, carry):
        body(i)
        return carry

    lax.fori_loop(0, count, step, 0)


def build_kernel(
    place, order, live, weight, depth_taps, row_taps, col_taps, images,
    depth_f, depth_a, row_f, row_a, col_f, col_a, *rest,
):
    slabs, ends = rest[:STEPS], rest[STEPS : 2 * STEPS]
    held, ahead, back, sems = rest[2 * STEPS :]
    copies = [
        pltpu.make_async_copy(images.at[0, step], slabs[step], sems.at[step])
        for step in range(STEPS)
    ]
    for copy in copies:
        copy.start()
    position, devices = place[0], place[1]
    for step in range(STEPS):
        block = lax.rem(position + (devices - step), devices)
        ends[step][0] = jnp.full((1, COLS), (block > 0).astype(F32))
        ends[step][1] = jnp.full((1, COLS), (block < devices - 1).astype(F32))
    views = order.shape[0]
    ranks, count = depth_taps.shape[1:]
    margin = count // 2
    view = order[lax.rem(position, views)]
    square = (TILE, TILE)

    def normal(taps):
        values = taps[view]
        return values / jnp.sum(values, axis=1, keepdims=True)

    rank = iota((ranks, 1), 0)
    weights = jnp.zeros((ranks, 1), F32)
    for r in range(ranks):
        weights = jnp.where(rank == r, weight[view, r], weights)
    weights = jnp.where(rank < live[view], weights, 0.0)
    weights = weights / jnp.sum(weights, axis=0, keepdims=True)

    def placed(values, place, to):
        held[...] = jnp.zeros(held.shape, F32)
        held[0:ranks, 0:count] = values
        k = iota((held.shape[1], TILE), 0)
        picks = (k < count) & (iota((held.shape[1], TILE), 1) == place(k))
        to[...] = dot(held[...].astype(BF16), picks.astype(F32).astype(BF16))

    def rolled(rows, r, n):
        full = jnp.broadcast_to(rows[pl.ds(r, 1)], (n, TILE))
        return pltpu.roll(full, 0, 1, stride=1, stride_axis=0)

    placed(normal(depth_taps) * weights, lambda k: GROUP * k, ahead)
    placed(normal(depth_taps) * weights, lambda k: GROUP * (count - 1 - k), back)

    def depth(r):
        depth_f[r] = rolled(ahead, r, PLANES * GROUP).astype(BF16)
        depth_a[r] = rolled(back, r, PLANES * GROUP).astype(BF16)

    loop(ranks, depth)
    i, j = iota(square, 0), iota(square, 1)
    near = jnp.abs(j - i) <= margin
    placed(normal(col_taps), lambda k: (margin - k) & (TILE - 1), ahead)
    placed(normal(col_taps), lambda k: (k - margin) & (TILE - 1), back)

    def col(r):
        col_f[r] = jnp.where(near, rolled(ahead, r, TILE), 0.0).astype(BF16)
        col_a[r] = jnp.where(near, rolled(back, r, TILE), 0.0).astype(BF16)

    loop(ranks, col)
    close = near & ((i >> 6) == (j >> 6))
    order_columns = ROWS * ((j >> 3) & (QUAD - 1)) + GROUP * (j >> 5) + (j & (GROUP - 1))
    order_columns = (i == order_columns).astype(F32).astype(BF16)
    placed(normal(row_taps), lambda k: (k - margin) & (TILE - 1), ahead)
    placed(normal(row_taps), lambda k: (margin - k) & (TILE - 1), back)

    def row(r):
        band = jnp.where(close, rolled(ahead, r, TILE), 0.0).astype(BF16)
        row_f[r] = dot(band, order_columns).astype(BF16)
        band = jnp.where(close, rolled(back, r, TILE), 0.0).astype(BF16)
        row_a[r] = dot(band, order_columns).astype(BF16)

    loop(ranks, row)
    for copy in copies:
        copy.wait()


def build(place, view_order, psf_ranks, rank_weight, depth_taps, row_taps, col_taps, images):
    ranks = depth_taps.shape[1]
    depth = jax.ShapeDtypeStruct((ranks, PLANES * GROUP, TILE), BF16)
    square = jax.ShapeDtypeStruct((ranks, TILE, TILE), BF16)
    slab = jax.ShapeDtypeStruct(images.shape[2:], BF16)
    ends = jax.ShapeDtypeStruct((2, 1, COLS), F32)
    out = pl.pallas_call(
        build_kernel,
        out_shape=[depth, depth] + [square] * 4 + [slab] * STEPS + [ends] * STEPS,
        in_specs=[SMEM] * 4 + [VMEM] * 3 + [HBM],
        out_specs=[VMEM] * (6 + 2 * STEPS),
        scratch_shapes=[
            pltpu.VMEM((8, 128), F32),
            pltpu.VMEM((8, TILE), F32),
            pltpu.VMEM((8, TILE), F32),
            pltpu.SemaphoreType.DMA((STEPS,)),
        ],
        compiler_params=pltpu.CompilerParams(vmem_limit_bytes=20 * 2**20),
        name="build",
    )(place, view_order, psf_ranks, rank_weight, depth_taps, row_taps, col_taps, images)
    return out[:6], out[6 : 6 + STEPS], out[6 + STEPS :]


def depth_pass(cells_of, op, planes, spread):
    ranks = op.shape[0]
    groups = ROWS // GROUP // 4
    lhs = op[:, 0 : planes * GROUP, :].reshape(ranks * planes * GROUP, TILE)

    def half(i):
        for g in range(groups):
            at = pl.multiple_of((i * groups + g) * GROUP, GROUP)
            cells = cells_of(pl.ds(at, GROUP))
            out = dot(lhs, cells.reshape(TILE, COLS).astype(BF16)).astype(BF16)
            out = out.reshape(ranks, planes // QUAD, QUAD * GROUP, COLS)
            to = pl.ds(pl.multiple_of(at * QUAD, QUAD * GROUP), QUAD * GROUP)
            spread[:, 0 : planes // QUAD, to, :] = out

    loop(4, half)


def row_pass(spread, op, mixed, t):
    rows = pl.ds(pl.multiple_of(t * TILE, TILE), TILE)
    for r in range(op.shape[0]):
        mixed[rows, r * COLS : (r + 1) * COLS] = dot(op[r], spread[r, t]).astype(BF16)


def col_pass(mixed, op, t):
    ranks = op.shape[0]
    rows = pl.ds(pl.multiple_of(t * TILE, TILE), TILE)
    return dot(mixed[rows, :], op[...].reshape(ranks * COLS, COLS)).reshape(QUAD, ROWS, COLS)


def depth_whole(cells_of, op, planes, spread):
    ranks = op.shape[0]
    lhs = op[:, 0 : planes * GROUP, :].reshape(ranks * planes * GROUP, TILE)
    for g in range(ROWS // GROUP):
        cells = cells_of(slice(g * GROUP, (g + 1) * GROUP))
        out = dot(lhs, cells.reshape(TILE, COLS).astype(BF16)).astype(BF16)
        out = out.reshape(ranks, planes // QUAD, QUAD * GROUP, COLS)
        spread[:, :, g * QUAD * GROUP : (g + 1) * QUAD * GROUP, :] = out


def row_whole(spread, op, mixed, t):
    for r in range(op.shape[0]):
        mixed[t * TILE : (t + 1) * TILE, r * COLS : (r + 1) * COLS] = dot(
            op[r], spread[r, t]
        ).astype(BF16)


def col_whole(mixed, op, t):
    ranks = op.shape[0]
    out = dot(mixed[t * TILE : (t + 1) * TILE, :], op[...].reshape(ranks * COLS, COLS))
    return out.reshape(QUAD, ROWS, COLS)


def window(refs, scales=None):
    def read(y):
        parts, left = [], 2 * PLANES
        for i, (ref, at) in enumerate(refs):
            n = min(left, ref.shape[0] - at)
            cells = ref[at : at + n, y, :]
            if scales is not None and scales[i] is not None:
                cells = cells * scales[i]
            parts.append(cells)
            left -= n
        while left > 0:
            n = min(left, parts[0].shape[0])
            parts.append(parts[0][:n])
            left -= n
        return jnp.concatenate(parts, axis=0)

    return read


def call(kernel, name, arrays, shared, ops, outs, scratch):
    out = [jax.ShapeDtypeStruct((n, ROWS, COLS), F32) for n in outs]
    return pl.pallas_call(
        kernel,
        out_shape=out,
        in_specs=[VMEM] * (len(arrays) + len(shared) + len(ops)),
        out_specs=[VMEM] * len(out),
        scratch_shapes=[pltpu.VMEM(shape, BF16) for shape in scratch],
        compiler_params=pltpu.CompilerParams(vmem_limit_bytes=20 * 2**20),
        cost_estimate=COST,
        name=name,
    )(*arrays, *shared, *ops)


def upper_ratio(own, above, shared, ops):
    parts = len(own) + len(above)
    tiles = PLANES // QUAD

    def kernel(*refs):
        slab, ends, depth, row, col, ratio, spread, mixed = refs[parts:]
        live = ends[1]
        scales = [None] * len(own) + [live] * len(above)
        cells = window([(ref, 0) for ref in refs[:parts]], scales)
        depth_pass(cells, depth, PLANES, spread)

        def pair(i):
            for t in (i,):
                row_pass(spread, row, mixed, t)
            for t in (i,):
                planes = pl.ds(t * QUAD, QUAD)
                seen = slab[pl.ds(PLANES + t * QUAD, QUAD)].astype(F32)
                ratio[planes] = seen / col_pass(mixed, col, t)

        loop(tiles, pair)
        ratio[HALF:] = ratio[HALF:] * live

    ranks = ops[0].shape[0]
    scratch = [(ranks, tiles, TILE, COLS), (tiles * TILE, ranks * COLS)]
    return call(kernel, "upper", own + above, shared, ops[0::2], [PLANES], scratch)[0]


def below_and_own(below, own, start):
    out = []
    for pieces, first in ((below, start), (own, 0)):
        at = 0
        for piece in pieces:
            n = piece.shape[0]
            if at + n > first:
                out.append((piece, max(first - at, 0)))
            at += n
    return out


def piece_update(start, below, own, ratios, shared, ops):
    sources = below_and_own(below, own, start)
    lower = sum(any(piece is p for p in below) for piece, _ in sources)
    parts = len(sources)
    given = parts + len(ratios)
    at = 0
    for i, piece in enumerate(own):
        if at <= start < at + piece.shape[0]:
            mine, offset = lower + i, start - at
        at += piece.shape[0]

    def kernel(*refs):
        slab, ends, depth_f, depth_a, row_f, row_a, col_f, col_a = refs[given : given + 8]
        ratio, updated, spread, mixed, spread_a, mixed_a = refs[given + 8 :]
        live = ends[0]
        depth = depth_whole if start in (0, PLANES - QUAD) else depth_pass
        scales = [live] * lower + [None] * (parts - lower)
        cells = window([(ref, at) for ref, (_, at) in zip(refs, sources)], scales)
        depth(cells, depth_f, QUAD, spread)
        row_whole(spread, row_f, mixed, 0)
        value = slab[start : start + QUAD].astype(F32) / col_whole(mixed, col_f, 0)
        ratio[...] = value * live if start < MARGIN else value
        cells = window([(ref, 0) for ref in (ratio,) + refs[parts:given]])
        depth(cells, depth_a, QUAD, spread_a)
        row_whole(spread_a, row_a, mixed_a, 0)
        updated[...] = refs[mine][offset : offset + QUAD] * col_whole(mixed_a, col_a, 0)

    ranks = ops[0].shape[0]
    scratch = [(ranks, 1, TILE, COLS), (TILE, ranks * COLS)] * 2
    arrays = [piece for piece, _ in sources] + ratios
    return call(kernel, "piece", arrays, shared, ops, [QUAD, QUAD], scratch)


def whole(pieces):
    def kernel(*refs):
        out, sems = refs[-2:]
        copies = [
            pltpu.make_async_copy(piece, out.at[pl.ds(i * QUAD, QUAD)], sems.at[i])
            for i, piece in enumerate(refs[:-2])
        ]
        for copy in copies:
            copy.start()
        for copy in copies:
            copy.wait()

    return pl.pallas_call(
        kernel,
        out_shape=jax.ShapeDtypeStruct((PLANES, ROWS, COLS), F32),
        in_specs=[VMEM] * len(pieces),
        out_specs=HBM,
        scratch_shapes=[pltpu.SemaphoreType.DMA((len(pieces),))],
        compiler_params=pltpu.CompilerParams(vmem_limit_bytes=20 * 2**20),
        cost_estimate=COST,
        name="whole",
    )(*pieces)


def shards(
    images, start_estimate, view_order, psf_ranks, depth_taps, row_taps, col_taps, rank_weight
):
    count = lax.axis_size("view")

    def send(cells, by, relayed=None, skip=()):
        pairs = []
        for i in range(count):
            way = relayed[1] if relayed and i % 4 == relayed[0] else by
            if i not in skip:
                pairs.append((i, (i + way) % count))
        return lax.ppermute(cells, "view", pairs)

    above = [send(start_estimate, -1)]
    place = jnp.stack([lax.axis_index("view"), count]).astype(jnp.int32)
    ops, slabs, ends = build(
        place, view_order, psf_ranks, rank_weight, depth_taps, row_taps, col_taps, images
    )
    own_lo, own_hi = start_estimate[:HALF], start_estimate[HALF:]
    early_hi, _ = lax.optimization_barrier((own_hi, ops[0]))
    below_hi = send(early_hi, 1, skip=(count - 1,))
    early_lo, _ = lax.optimization_barrier((own_lo, above[0]))
    below_lo = send(early_lo, 1, skip=(count - 1,))

    below, own = [below_lo, below_hi], [own_lo, own_hi]
    for step in range(STEPS):
        last = step == STEPS - 1
        shared = [slabs[step], ends[step]]
        ratios = [upper_ratio(own, above, shared, ops)]
        updated, arrived = [], []
        for start in range(PLANES - QUAD, -1, -QUAD):
            ratio, piece = piece_update(start, below, own, ratios, shared, ops)
            ratios = [ratio] + ratios
            updated = [piece] + updated
            relayed = (1, 1) if start >= HALF else None
            piece = send(piece, 1 - STEPS, relayed) if last else send(piece, 1)
            arrived = [piece] + arrived
        above, own = updated, arrived
        if not last:
            below = [send(piece, 1) for piece in own[::-1]][::-1]
    upper, _ = lax.optimization_barrier((own[HALF // QUAD :], updated[0]))
    return whole(own[: HALF // QUAD] + [send(piece, 0, (2, -STEPS)) for piece in upper])


def solution(mesh):
    in_specs = (
        P(("groups", "view"), None, None, None, None),
        P(("groups", "view"), None, None),
        P(),
        P(),
        P(),
        P(),
        P(),
        P(),
    )
    out_specs = P(("groups", "view"), None, None)
    return jax.shard_map(shards, mesh=mesh, in_specs=in_specs, out_specs=out_specs, check_vma=False)
```

```python
import jax
import jax.numpy as jnp
from jax import lax
from jax.experimental import pallas as pl
from jax.experimental.pallas import tpu as pltpu
from jax.sharding import PartitionSpec as P

STEPS = 4
PLANES = 16
MARGIN = 8
HALF = 8
ROWS = 64
COLS = 256
GROUP = 8
QUAD = 4
TILE = 256

F32 = jnp.float32
BF16 = jnp.bfloat16
VMEM = pl.BlockSpec(memory_space=pltpu.VMEM)
SMEM = pl.BlockSpec(memory_space=pltpu.SMEM)
COST = pl.CostEstimate(flops=2**20, bytes_accessed=2**10, transcendentals=0)
HBM = pl.BlockSpec(memory_space=pltpu.HBM)


def dot(a, b):
    return jnp.dot(a, b, preferred_element_type=F32)


def iota(shape, dim):
    return lax.broadcasted_iota(jnp.int32, shape, dim)


def loop(count, body):
    def step(i, carry):
        body(i)
        return carry

    lax.fori_loop(0, count, step, 0)


def build_kernel(
    place, order, live, weight, depth_taps, row_taps, col_taps, images,
    depth_f, depth_a, row_f, row_a, col_f, col_a, *rest,
):
    slabs, ends = rest[:STEPS], rest[STEPS : 2 * STEPS]
    held, ahead, back, sems = rest[2 * STEPS :]
    copies = [
        pltpu.make_async_copy(images.at[0, step], slabs[step], sems.at[step])
        for step in range(STEPS)
    ]
    for copy in copies:
        copy.start()
    position, devices = place[0], place[1]
    for step in range(STEPS):
        block = lax.rem(position + (devices - step), devices)
        ends[step][0] = jnp.full((1, COLS), (block > 0).astype(F32))
        ends[step][1] = jnp.full((1, COLS), (block < devices - 1).astype(F32))
    views = order.shape[0]
    ranks, count = depth_taps.shape[1:]
    margin = count // 2
    view = order[lax.rem(position, views)]
    square = (TILE, TILE)

    def normal(taps):
        values = taps[view]
        return values / jnp.sum(values, axis=1, keepdims=True)

    rank = iota((ranks, 1), 0)
    weights = jnp.zeros((ranks, 1), F32)
    for r in range(ranks):
        weights = jnp.where(rank == r, weight[view, r], weights)
    weights = jnp.where(rank < live[view], weights, 0.0)
    weights = weights / jnp.sum(weights, axis=0, keepdims=True)

    def placed(values, place, to):
        held[...] = jnp.zeros(held.shape, F32)
        held[0:ranks, 0:count] = values
        k = iota((held.shape[1], TILE), 0)
        picks = (k < count) & (iota((held.shape[1], TILE), 1) == place(k))
        to[...] = dot(held[...].astype(BF16), picks.astype(F32).astype(BF16))

    def rolled(rows, r, n):
        full = jnp.broadcast_to(rows[pl.ds(r, 1)], (n, TILE))
        return pltpu.roll(full, 0, 1, stride=1, stride_axis=0)

    placed(normal(depth_taps) * weights, lambda k: GROUP * k, ahead)
    placed(normal(depth_taps) * weights, lambda k: GROUP * (count - 1 - k), back)

    def depth(r):
        depth_f[r] = rolled(ahead, r, PLANES * GROUP).astype(BF16)
        depth_a[r] = rolled(back, r, PLANES * GROUP).astype(BF16)

    for r in range(ranks):
        depth(r)
    i, j = iota(square, 0), iota(square, 1)
    near = jnp.abs(j - i) <= margin
    placed(normal(col_taps), lambda k: (margin - k) & (TILE - 1), ahead)
    placed(normal(col_taps), lambda k: (k - margin) & (TILE - 1), back)

    def col(r):
        col_f[r] = jnp.where(near, rolled(ahead, r, TILE), 0.0).astype(BF16)
        col_a[r] = jnp.where(near, rolled(back, r, TILE), 0.0).astype(BF16)

    for r in range(ranks):
        col(r)
    close = near & ((i >> 6) == (j >> 6))
    order_columns = ROWS * ((j >> 3) & (QUAD - 1)) + GROUP * (j >> 5) + (j & (GROUP - 1))
    order_columns = (i == order_columns).astype(F32).astype(BF16)
    placed(normal(row_taps), lambda k: (k - margin) & (TILE - 1), ahead)
    placed(normal(row_taps), lambda k: (margin - k) & (TILE - 1), back)

    def row(r):
        band = jnp.where(close, rolled(ahead, r, TILE), 0.0).astype(BF16)
        row_f[r] = dot(band, order_columns).astype(BF16)
        band = jnp.where(close, rolled(back, r, TILE), 0.0).astype(BF16)
        row_a[r] = dot(band, order_columns).astype(BF16)

    for r in range(ranks):
        row(r)
    for copy in copies:
        copy.wait()


def build(place, view_order, psf_ranks, rank_weight, depth_taps, row_taps, col_taps, images):
    ranks = depth_taps.shape[1]
    depth = jax.ShapeDtypeStruct((ranks, PLANES * GROUP, TILE), BF16)
    square = jax.ShapeDtypeStruct((ranks, TILE, TILE), BF16)
    slab = jax.ShapeDtypeStruct(images.shape[2:], BF16)
    ends = jax.ShapeDtypeStruct((2, 1, COLS), F32)
    out = pl.pallas_call(
        build_kernel,
        out_shape=[depth, depth] + [square] * 4 + [slab] * STEPS + [ends] * STEPS,
        in_specs=[SMEM] * 4 + [VMEM] * 3 + [HBM],
        out_specs=[VMEM] * (6 + 2 * STEPS),
        scratch_shapes=[
            pltpu.VMEM((8, 128), F32),
            pltpu.VMEM((8, TILE), F32),
            pltpu.VMEM((8, TILE), F32),
            pltpu.SemaphoreType.DMA((STEPS,)),
        ],
        compiler_params=pltpu.CompilerParams(vmem_limit_bytes=20 * 2**20),
        name="build",
    )(place, view_order, psf_ranks, rank_weight, depth_taps, row_taps, col_taps, images)
    return out[:6], out[6 : 6 + STEPS], out[6 + STEPS :]


def depth_pass(cells_of, op, planes, spread):
    ranks = op.shape[0]
    groups = ROWS // GROUP // 4
    lhs = op[:, 0 : planes * GROUP, :].reshape(ranks * planes * GROUP, TILE)

    def half(i):
        for g in range(groups):
            at = pl.multiple_of((i * groups + g) * GROUP, GROUP)
            cells = cells_of(pl.ds(at, GROUP))
            out = dot(lhs, cells.reshape(TILE, COLS).astype(BF16)).astype(BF16)
            out = out.reshape(ranks, planes // QUAD, QUAD * GROUP, COLS)
            to = pl.ds(pl.multiple_of(at * QUAD, QUAD * GROUP), QUAD * GROUP)
            spread[:, 0 : planes // QUAD, to, :] = out

    loop(4, half)


def row_pass(spread, op, mixed, t):
    rows = pl.ds(pl.multiple_of(t * TILE, TILE), TILE)
    for r in range(op.shape[0]):
        mixed[rows, r * COLS : (r + 1) * COLS] = dot(op[r], spread[r, t]).astype(BF16)


def col_pass(mixed, op, t):
    ranks = op.shape[0]
    rows = pl.ds(pl.multiple_of(t * TILE, TILE), TILE)
    return dot(mixed[rows, :], op[...].reshape(ranks * COLS, COLS)).reshape(QUAD, ROWS, COLS)


def depth_whole(cells_of, op, planes, spread):
    ranks = op.shape[0]
    lhs = op[:, 0 : planes * GROUP, :].reshape(ranks * planes * GROUP, TILE)
    for g in range(ROWS // GROUP):
        cells = cells_of(slice(g * GROUP, (g + 1) * GROUP))
        out = dot(lhs, cells.reshape(TILE, COLS).astype(BF16)).astype(BF16)
        out = out.reshape(ranks, planes // QUAD, QUAD * GROUP, COLS)
        spread[:, :, g * QUAD * GROUP : (g + 1) * QUAD * GROUP, :] = out


def row_whole(spread, op, mixed, t):
    for r in range(op.shape[0]):
        mixed[t * TILE : (t + 1) * TILE, r * COLS : (r + 1) * COLS] = dot(
            op[r], spread[r, t]
        ).astype(BF16)


def col_whole(mixed, op, t):
    ranks = op.shape[0]
    out = dot(mixed[t * TILE : (t + 1) * TILE, :], op[...].reshape(ranks * COLS, COLS))
    return out.reshape(QUAD, ROWS, COLS)


def window(refs, scales=None):
    def read(y):
        parts, left = [], 2 * PLANES
        for i, (ref, at) in enumerate(refs):
            n = min(left, ref.shape[0] - at)
            cells = ref[at : at + n, y, :]
            if scales is not None and scales[i] is not None:
                cells = cells * scales[i]
            parts.append(cells)
            left -= n
        while left > 0:
            n = min(left, parts[0].shape[0])
            parts.append(parts[0][:n])
            left -= n
        return jnp.concatenate(parts, axis=0)

    return read


def call(kernel, name, arrays, shared, ops, outs, scratch):
    out = [jax.ShapeDtypeStruct((n, ROWS, COLS), F32) for n in outs]
    return pl.pallas_call(
        kernel,
        out_shape=out,
        in_specs=[VMEM] * (len(arrays) + len(shared) + len(ops)),
        out_specs=[VMEM] * len(out),
        scratch_shapes=[pltpu.VMEM(shape, BF16) for shape in scratch],
        compiler_params=pltpu.CompilerParams(vmem_limit_bytes=20 * 2**20),
        cost_estimate=COST,
        name=name,
    )(*arrays, *shared, *ops)


def upper_ratio(own, above, shared, ops, unrolled):
    parts = len(own) + len(above)
    tiles = PLANES // QUAD

    def kernel(*refs):
        slab, ends, depth, row, col, ratio, spread, mixed = refs[parts:]
        live = ends[1]
        scales = [None] * len(own) + [live] * len(above)
        cells = window([(ref, 0) for ref in refs[:parts]], scales)
        (depth_whole if unrolled else depth_pass)(cells, depth, PLANES, spread)

        def pair(i):
            for t in (i,):
                row_pass(spread, row, mixed, t)
            for t in (i,):
                planes = pl.ds(t * QUAD, QUAD)
                seen = slab[pl.ds(PLANES + t * QUAD, QUAD)].astype(F32)
                ratio[planes] = seen / col_pass(mixed, col, t)

        if unrolled:
            for t in range(tiles):
                row_whole(spread, row, mixed, t)
            for t in range(tiles):
                seen = slab[PLANES + t * QUAD : PLANES + (t + 1) * QUAD].astype(F32)
                ratio[t * QUAD : (t + 1) * QUAD] = seen / col_whole(mixed, col, t)
        else:
            loop(tiles, pair)
        ratio[HALF:] = ratio[HALF:] * live

    ranks = ops[0].shape[0]
    scratch = [(ranks, tiles, TILE, COLS), (tiles * TILE, ranks * COLS)]
    return call(kernel, "upper", own + above, shared, ops[0::2], [PLANES], scratch)[0]


def half_update(start, below, own, ratios, shared, ops):
    parts = len(below) + len(own)
    given = parts + len(ratios)

    def kernel(*refs):
        slab, ends, depth_f, depth_a, row_f, row_a, col_f, col_a = refs[given : given + 8]
        ratio, updated, spread, mixed, spread_hi, mixed_hi, spread_lo, mixed_lo = refs[given + 8 :]
        live = ends[0]
        scales = [live] * len(below) + [None] * len(own)

        def divide(t):
            planes = slice(t * QUAD, (t + 1) * QUAD)
            seen = slab[start + t * QUAD : start + (t + 1) * QUAD].astype(F32)
            value = seen / col_whole(mixed, col_f, t)
            ratio[planes] = value * live if start == 0 else value

        def back(t, mixed_t):
            planes = slice(t * QUAD, (t + 1) * QUAD)
            updated[planes] = refs[parts - 1][planes] * col_whole(mixed_t, col_a, 0)

        ratio_refs = [(ref, 0) for ref in refs[parts:given]]
        depth_whole(window([(ref, 0) for ref in refs[:parts]], scales), depth_f, HALF, spread)
        row_whole(spread, row_f, mixed, 1)
        divide(1)
        row_whole(spread, row_f, mixed, 0)
        depth_whole(window([(ratio, QUAD)] + ratio_refs), depth_a, QUAD, spread_hi)
        divide(0)
        row_whole(spread_hi, row_a, mixed_hi, 0)
        depth_whole(window([(ratio, 0)] + ratio_refs), depth_a, QUAD, spread_lo)
        back(1, mixed_hi)
        row_whole(spread_lo, row_a, mixed_lo, 0)
        back(0, mixed_lo)

    ranks = ops[0].shape[0]
    scratch = [
        shape
        for tiles in (2, 1, 1)
        for shape in ((ranks, tiles, TILE, COLS), (tiles * TILE, ranks * COLS))
    ]
    return call(kernel, "half", below + own + ratios, shared, ops, [HALF, HALF], scratch)


def whole(lo, hi):
    def kernel(lo, hi, out, sems):
        copies = [
            pltpu.make_async_copy(half, out.at[pl.ds(i * HALF, HALF)], sems.at[i])
            for i, half in enumerate((lo, hi))
        ]
        for copy in copies:
            copy.start()
        for copy in copies:
            copy.wait()

    return pl.pallas_call(
        kernel,
        out_shape=jax.ShapeDtypeStruct((PLANES, ROWS, COLS), F32),
        in_specs=[VMEM] * 2,
        out_specs=HBM,
        scratch_shapes=[pltpu.SemaphoreType.DMA((2,))],
        compiler_params=pltpu.CompilerParams(vmem_limit_bytes=20 * 2**20),
        cost_estimate=COST,
        name="whole",
    )(lo, hi)


def shards(
    images, start_estimate, view_order, psf_ranks, depth_taps, row_taps, col_taps, rank_weight
):
    count = lax.axis_size("view")

    def send(cells, by, relayed=None, skip=()):
        pairs = []
        for i in range(count):
            way = relayed[1] if relayed and i % 4 == relayed[0] else by
            if i not in skip:
                pairs.append((i, (i + way) % count))
        return lax.ppermute(cells, "view", pairs)

    above = [send(start_estimate, -1, skip=(0,))]
    place = jnp.stack([lax.axis_index("view"), count]).astype(jnp.int32)
    ops, slabs, ends = build(
        place, view_order, psf_ranks, rank_weight, depth_taps, row_taps, col_taps, images
    )
    own_lo, own_hi = start_estimate[:HALF], start_estimate[HALF:]
    early_hi, _ = lax.optimization_barrier((own_hi, ops[0]))
    below_hi = send(early_hi, 1, skip=(count - 1,))
    early_lo, _ = lax.optimization_barrier((own_lo, above[0]))
    below_lo = send(early_lo, 1, skip=(count - 1,))

    for step in range(STEPS):
        last = step == STEPS - 1
        shared = [slabs[step], ends[step]]
        ratio_up = upper_ratio([own_lo, own_hi], above, shared, ops, step == 0)
        ratio_mid, hi = half_update(HALF, [below_hi], [own_lo, own_hi], [ratio_up], shared, ops)
        next_hi = send(hi, 1 - STEPS, (1, 1)) if last else send(hi, 1)
        _, lo = half_update(
            0, [below_lo, below_hi], [own_lo], [ratio_mid, ratio_up], shared, ops
        )
        above = [lo, hi]
        if last:
            next_hi, _ = lax.optimization_barrier((next_hi, lo))
            own_lo = send(lo, 1 - STEPS)
            own_hi = send(next_hi, 0, (2, -STEPS))
        else:
            own_lo, own_hi = send(lo, 1), next_hi
            below_hi = send(own_hi, 1)
            below_lo = send(own_lo, 1)
    return whole(own_lo, own_hi)


def solution(mesh):
    in_specs = (
        P(("groups", "view"), None, None, None, None),
        P(("groups", "view"), None, None),
        P(),
        P(),
        P(),
        P(),
        P(),
        P(),
    )
    out_specs = P(("groups", "view"), None, None)
    return jax.shard_map(shards, mesh=mesh, in_specs=in_specs, out_specs=out_specs, check_vma=False)
```

```python
import jax
import jax.numpy as jnp
from jax import lax
from jax.experimental import pallas as pl
from jax.experimental.pallas import tpu as pltpu
from jax.sharding import PartitionSpec as P

STEPS = 4
PLANES = 16
MARGIN = 8
HALF = 8
ROWS = 64
COLS = 256
GROUP = 8
QUAD = 4
TILE = 256

F32 = jnp.float32
BF16 = jnp.bfloat16
VMEM = pl.BlockSpec(memory_space=pltpu.VMEM)
SMEM = pl.BlockSpec(memory_space=pltpu.SMEM)
COST = pl.CostEstimate(flops=2**20, bytes_accessed=2**10, transcendentals=0)
HBM = pl.BlockSpec(memory_space=pltpu.HBM)


def dot(a, b):
    return jnp.dot(a, b, preferred_element_type=F32)


def iota(shape, dim):
    return lax.broadcasted_iota(jnp.int32, shape, dim)


def loop(count, body):
    def step(i, carry):
        body(i)
        return carry

    lax.fori_loop(0, count, step, 0)


def build_kernel(
    place, order, live, weight, depth_taps, row_taps, col_taps, images,
    depth_f, depth_a, row_f, row_a, col_f, col_a, *rest,
):
    slabs, ends = rest[:STEPS], rest[STEPS : 2 * STEPS]
    held, ahead, back, sems = rest[2 * STEPS :]
    copies = [
        pltpu.make_async_copy(images.at[0, step], slabs[step], sems.at[step])
        for step in range(STEPS)
    ]
    for copy in copies:
        copy.start()
    position, devices = place[0], place[1]
    for step in range(STEPS):
        block = lax.rem(position + (devices - step), devices)
        ends[step][0] = jnp.full((1, COLS), (block > 0).astype(F32))
        ends[step][1] = jnp.full((1, COLS), (block < devices - 1).astype(F32))
    views = order.shape[0]
    ranks, count = depth_taps.shape[1:]
    margin = count // 2
    view = order[lax.rem(position, views)]
    square = (TILE, TILE)

    def normal(taps):
        values = taps[view]
        return values / jnp.sum(values, axis=1, keepdims=True)

    rank = iota((ranks, 1), 0)
    weights = jnp.zeros((ranks, 1), F32)
    for r in range(ranks):
        weights = jnp.where(rank == r, weight[view, r], weights)
    weights = jnp.where(rank < live[view], weights, 0.0)
    weights = weights / jnp.sum(weights, axis=0, keepdims=True)

    def placed(values, place, to):
        held[...] = jnp.zeros(held.shape, F32)
        held[0:ranks, 0:count] = values
        k = iota((held.shape[1], TILE), 0)
        picks = (k < count) & (iota((held.shape[1], TILE), 1) == place(k))
        to[...] = dot(held[...].astype(BF16), picks.astype(F32).astype(BF16))

    def rolled(rows, r, n):
        full = jnp.broadcast_to(rows[pl.ds(r, 1)], (n, TILE))
        return pltpu.roll(full, 0, 1, stride=1, stride_axis=0)

    placed(normal(depth_taps) * weights, lambda k: GROUP * k, ahead)
    placed(normal(depth_taps) * weights, lambda k: GROUP * (count - 1 - k), back)

    def depth(r):
        depth_f[r] = rolled(ahead, r, PLANES * GROUP).astype(BF16)
        depth_a[r] = rolled(back, r, PLANES * GROUP).astype(BF16)

    for r in range(ranks):
        depth(r)
    i, j = iota(square, 0), iota(square, 1)
    near = jnp.abs(j - i) <= margin
    placed(normal(col_taps), lambda k: (margin - k) & (TILE - 1), ahead)
    placed(normal(col_taps), lambda k: (k - margin) & (TILE - 1), back)

    def col(r):
        col_f[r] = jnp.where(near, rolled(ahead, r, TILE), 0.0).astype(BF16)
        col_a[r] = jnp.where(near, rolled(back, r, TILE), 0.0).astype(BF16)

    for r in range(ranks):
        col(r)
    close = near & ((i >> 6) == (j >> 6))
    order_columns = ROWS * ((j >> 3) & (QUAD - 1)) + GROUP * (j >> 5) + (j & (GROUP - 1))
    order_columns = (i == order_columns).astype(F32).astype(BF16)
    placed(normal(row_taps), lambda k: (k - margin) & (TILE - 1), ahead)
    placed(normal(row_taps), lambda k: (margin - k) & (TILE - 1), back)

    def row(r):
        band = jnp.where(close, rolled(ahead, r, TILE), 0.0).astype(BF16)
        row_f[r] = dot(band, order_columns).astype(BF16)
        band = jnp.where(close, rolled(back, r, TILE), 0.0).astype(BF16)
        row_a[r] = dot(band, order_columns).astype(BF16)

    for r in range(ranks):
        row(r)
    for copy in copies:
        copy.wait()


def build(place, view_order, psf_ranks, rank_weight, depth_taps, row_taps, col_taps, images):
    ranks = depth_taps.shape[1]
    depth = jax.ShapeDtypeStruct((ranks, PLANES * GROUP, TILE), BF16)
    square = jax.ShapeDtypeStruct((ranks, TILE, TILE), BF16)
    slab = jax.ShapeDtypeStruct(images.shape[2:], BF16)
    ends = jax.ShapeDtypeStruct((2, 1, COLS), F32)
    out = pl.pallas_call(
        build_kernel,
        out_shape=[depth, depth] + [square] * 4 + [slab] * STEPS + [ends] * STEPS,
        in_specs=[SMEM] * 4 + [VMEM] * 3 + [HBM],
        out_specs=[VMEM] * (6 + 2 * STEPS),
        scratch_shapes=[
            pltpu.VMEM((8, 128), F32),
            pltpu.VMEM((8, TILE), F32),
            pltpu.VMEM((8, TILE), F32),
            pltpu.SemaphoreType.DMA((STEPS,)),
        ],
        compiler_params=pltpu.CompilerParams(vmem_limit_bytes=20 * 2**20),
        name="build",
    )(place, view_order, psf_ranks, rank_weight, depth_taps, row_taps, col_taps, images)
    return out[:6], out[6 : 6 + STEPS], out[6 + STEPS :]


def depth_pass(cells_of, op, planes, spread):
    ranks = op.shape[0]
    groups = ROWS // GROUP // 4
    lhs = op[:, 0 : planes * GROUP, :].reshape(ranks * planes * GROUP, TILE)

    def half(i):
        for g in range(groups):
            at = pl.multiple_of((i * groups + g) * GROUP, GROUP)
            cells = cells_of(pl.ds(at, GROUP))
            out = dot(lhs, cells.reshape(TILE, COLS).astype(BF16)).astype(BF16)
            out = out.reshape(ranks, planes // QUAD, QUAD * GROUP, COLS)
            to = pl.ds(pl.multiple_of(at * QUAD, QUAD * GROUP), QUAD * GROUP)
            spread[:, 0 : planes // QUAD, to, :] = out

    loop(4, half)


def row_pass(spread, op, mixed, t):
    rows = pl.ds(pl.multiple_of(t * TILE, TILE), TILE)
    for r in range(op.shape[0]):
        mixed[rows, r * COLS : (r + 1) * COLS] = dot(op[r], spread[r, t]).astype(BF16)


def col_pass(mixed, op, t):
    ranks = op.shape[0]
    rows = pl.ds(pl.multiple_of(t * TILE, TILE), TILE)
    return dot(mixed[rows, :], op[...].reshape(ranks * COLS, COLS)).reshape(QUAD, ROWS, COLS)


def depth_whole(cells_of, op, planes, spread):
    ranks = op.shape[0]
    lhs = op[:, 0 : planes * GROUP, :].reshape(ranks * planes * GROUP, TILE)
    for g in range(ROWS // GROUP):
        cells = cells_of(slice(g * GROUP, (g + 1) * GROUP))
        out = dot(lhs, cells.reshape(TILE, COLS).astype(BF16)).astype(BF16)
        out = out.reshape(ranks, planes // QUAD, QUAD * GROUP, COLS)
        spread[:, :, g * QUAD * GROUP : (g + 1) * QUAD * GROUP, :] = out


def row_whole(spread, op, mixed, t):
    for r in range(op.shape[0]):
        mixed[t * TILE : (t + 1) * TILE, r * COLS : (r + 1) * COLS] = dot(
            op[r], spread[r, t]
        ).astype(BF16)


def col_whole(mixed, op, t):
    ranks = op.shape[0]
    out = dot(mixed[t * TILE : (t + 1) * TILE, :], op[...].reshape(ranks * COLS, COLS))
    return out.reshape(QUAD, ROWS, COLS)


def window(refs, scales=None):
    def read(y):
        parts, left = [], 2 * PLANES
        for i, (ref, at) in enumerate(refs):
            n = min(left, ref.shape[0] - at)
            cells = ref[at : at + n, y, :]
            if scales is not None and scales[i] is not None:
                cells = cells * scales[i]
            parts.append(cells)
            left -= n
        while left > 0:
            n = min(left, parts[0].shape[0])
            parts.append(parts[0][:n])
            left -= n
        return jnp.concatenate(parts, axis=0)

    return read


def call(kernel, name, arrays, shared, ops, outs, scratch):
    out = [jax.ShapeDtypeStruct((n, ROWS, COLS), F32) for n in outs]
    return pl.pallas_call(
        kernel,
        out_shape=out,
        in_specs=[VMEM] * (len(arrays) + len(shared) + len(ops)),
        out_specs=[VMEM] * len(out),
        scratch_shapes=[pltpu.VMEM(shape, BF16) for shape in scratch],
        compiler_params=pltpu.CompilerParams(vmem_limit_bytes=20 * 2**20),
        cost_estimate=COST,
        name=name,
    )(*arrays, *shared, *ops)


def upper_ratio(own, above, shared, ops, unrolled):
    parts = len(own) + len(above)
    tiles = PLANES // QUAD

    def kernel(*refs):
        slab, ends, depth, row, col, ratio, spread, mixed = refs[parts:]
        live = ends[1]
        scales = [None] * len(own) + [live] * len(above)
        cells = window([(ref, 0) for ref in refs[:parts]], scales)
        (depth_whole if unrolled else depth_pass)(cells, depth, PLANES, spread)

        def pair(i):
            for t in (i,):
                row_pass(spread, row, mixed, t)
            for t in (i,):
                planes = pl.ds(t * QUAD, QUAD)
                seen = slab[pl.ds(PLANES + t * QUAD, QUAD)].astype(F32)
                ratio[planes] = seen / col_pass(mixed, col, t)

        if unrolled:
            for t in range(tiles):
                row_whole(spread, row, mixed, t)
            for t in range(tiles):
                seen = slab[PLANES + t * QUAD : PLANES + (t + 1) * QUAD].astype(F32)
                ratio[t * QUAD : (t + 1) * QUAD] = seen / col_whole(mixed, col, t)
        else:
            loop(tiles, pair)
        ratio[HALF:] = ratio[HALF:] * live

    ranks = ops[0].shape[0]
    scratch = [(ranks, tiles, TILE, COLS), (tiles * TILE, ranks * COLS)]
    return call(kernel, "upper", own + above, shared, ops[0::2], [PLANES], scratch)[0]


def half_update(start, below, own, ratios, shared, ops):
    parts = len(below) + len(own)
    given = parts + len(ratios)

    def kernel(*refs):
        slab, ends, depth_f, depth_a, row_f, row_a, col_f, col_a = refs[given : given + 8]
        ratio, updated, spread, mixed, spread_f, mixed_f = refs[given + 8 : given + 14]
        spread_hi, mixed_hi, spread_lo, mixed_lo = refs[given + 14 :]
        live = ends[0]
        scales = [live] * len(below) + [None] * len(own)

        def divide(t, mixed_t):
            planes = slice(t * QUAD, (t + 1) * QUAD)
            seen = slab[start + t * QUAD : start + (t + 1) * QUAD].astype(F32)
            value = seen / col_whole(mixed_t, col_f, 0)
            ratio[planes] = value * live if start == 0 else value

        def back(t, mixed_t):
            planes = slice(t * QUAD, (t + 1) * QUAD)
            updated[planes] = refs[parts - 1][planes] * col_whole(mixed_t, col_a, 0)

        ratio_refs = [(ref, 0) for ref in refs[parts:given]]
        above_first = [(ref, 0) for ref in refs[1:parts]]
        depth_whole(window([(refs[0], QUAD)] + above_first, scales), depth_f, QUAD, spread)
        row_whole(spread, row_f, mixed, 0)
        depth_whole(window([(refs[0], 0)] + above_first, scales), depth_f, QUAD, spread_f)
        divide(1, mixed)
        row_whole(spread_f, row_f, mixed_f, 0)
        depth_whole(window([(ratio, QUAD)] + ratio_refs), depth_a, QUAD, spread_hi)
        divide(0, mixed_f)
        row_whole(spread_hi, row_a, mixed_hi, 0)
        depth_whole(window([(ratio, 0)] + ratio_refs), depth_a, QUAD, spread_lo)
        back(1, mixed_hi)
        row_whole(spread_lo, row_a, mixed_lo, 0)
        back(0, mixed_lo)

    ranks = ops[0].shape[0]
    scratch = [(ranks, 1, TILE, COLS), (TILE, ranks * COLS)] * 4
    return call(kernel, "half", below + own + ratios, shared, ops, [HALF, HALF], scratch)


def whole(lo, hi):
    def kernel(lo, hi, out, sems):
        copies = [
            pltpu.make_async_copy(half, out.at[pl.ds(i * HALF, HALF)], sems.at[i])
            for i, half in enumerate((lo, hi))
        ]
        for copy in copies:
            copy.start()
        for copy in copies:
            copy.wait()

    return pl.pallas_call(
        kernel,
        out_shape=jax.ShapeDtypeStruct((PLANES, ROWS, COLS), F32),
        in_specs=[VMEM] * 2,
        out_specs=HBM,
        scratch_shapes=[pltpu.SemaphoreType.DMA((2,))],
        compiler_params=pltpu.CompilerParams(vmem_limit_bytes=20 * 2**20),
        cost_estimate=COST,
        name="whole",
    )(lo, hi)


def shards(
    images, start_estimate, view_order, psf_ranks, depth_taps, row_taps, col_taps, rank_weight
):
    count = lax.axis_size("view")

    def send(cells, by, relayed=None, skip=()):
        pairs = []
        for i in range(count):
            way = relayed[1] if relayed and i % 4 == relayed[0] else by
            if i not in skip:
                pairs.append((i, (i + way) % count))
        return lax.ppermute(cells, "view", pairs)

    above = [send(start_estimate, -1, skip=(0,))]
    place = jnp.stack([lax.axis_index("view"), count]).astype(jnp.int32)
    ops, slabs, ends = build(
        place, view_order, psf_ranks, rank_weight, depth_taps, row_taps, col_taps, images
    )
    own_lo, own_hi = start_estimate[:HALF], start_estimate[HALF:]
    early_hi, _ = lax.optimization_barrier((own_hi, ops[0]))
    below_hi = send(early_hi, 1, skip=(count - 1,))
    early_lo, _ = lax.optimization_barrier((own_lo, above[0]))
    below_lo = send(early_lo, 1, skip=(count - 1,))

    for step in range(STEPS):
        last = step == STEPS - 1
        shared = [slabs[step], ends[step]]
        ratio_up = upper_ratio([own_lo, own_hi], above, shared, ops, step == 0)
        ratio_mid, hi = half_update(HALF, [below_hi], [own_lo, own_hi], [ratio_up], shared, ops)
        next_hi = send(hi, 1 - STEPS, (1, 1)) if last else send(hi, 1)
        _, lo = half_update(
            0, [below_lo, below_hi], [own_lo], [ratio_mid, ratio_up], shared, ops
        )
        above = [lo, hi]
        if last:
            next_hi, _ = lax.optimization_barrier((next_hi, lo))
            own_lo = send(lo, 1 - STEPS)
            own_hi = send(next_hi, 0, (2, -STEPS))
        else:
            own_lo, own_hi = send(lo, 1), next_hi
            below_hi = send(own_hi, 1)
            below_lo = send(own_lo, 1)
    return whole(own_lo, own_hi)


def solution(mesh):
    in_specs = (
        P(("groups", "view"), None, None, None, None),
        P(("groups", "view"), None, None),
        P(),
        P(),
        P(),
        P(),
        P(),
        P(),
    )
    out_specs = P(("groups", "view"), None, None)
    return jax.shard_map(shards, mesh=mesh, in_specs=in_specs, out_specs=out_specs, check_vma=False)
```
